256 devices in a mesh: grp: 4 (over x_hi, core), dev: 64 (over x_lo, y, z).
Axes of the slice: x: 4 (x_hi: 2, x_lo: 2; x = x_hi * 2 + x_lo), y: 4, z: 8, core: 2. Of those that a mesh axis runs over, the one named last changes fastest.
Arguments:
- hidden_in: bfloat16 [32, 5120], P('grp', 'dev'), may hold values from -6 to 6
- w_qkv: bfloat16 [5120, 7168], P(None, ('grp', 'dev')), may hold values from -0.078125 to 0.078125
- w_o: bfloat16 [5120, 5120], P(None, ('grp', 'dev')), may hold values from -0.3125 to 0.3125
- key_cache: bfloat16 [32, 8192, 1024], P('grp', 'dev'), may hold values from -144 to 144
- value_cache: bfloat16 [32, 8192, 1024], P('grp', 'dev'), may hold values from -6 to 6
- lengths: int32 [32], P('grp'), may hold values from 1 to 8192, as said below
- finished: int32 [32], P('grp'), may hold values from 0 to 1, as said below
- assignment: int32 [32], P('grp'), may hold values from 0 to 3, as said below
Outputs:
- hidden_out: float32 [32, 5120], P('grp', 'dev')
- returned: float32 [32, 5120], P('grp', 'dev')
- w_qkv_gen: bfloat16 [5120, 7168], P('dev')
- w_o_gen: bfloat16 [5120, 5120], P('dev')
The draws below stay inside these ranges and needn't reach their ends.
Inputs may be any that keep to these rules, and one draw needn't show every extreme that they name: `lengths`: some row has exactly 8192. `assignment`: within each generator group every learner shard is named by exactly 2 rows. One learner shard, the same for all generator groups, has all its 2 rows finished in every group.
All inputs are finite; a program needn't handle non-finite values.
Results may differ from the reference program's by a relative error of at most 0.028.
Values may be sent and summed in bfloat16 or wider, within the bound.
No kernel may reach another device: no remote copies, remote signals or barrier semaphores. Data moves between devices by JAX's collectives and lax.ppermute only.
A program may use at most 64 MiB of HBM per device.

```python
import math
import jax
import jax.numpy as jnp
from jax import lax

D = 5120
QUERY_HEADS = 40
KEY_VALUE_HEADS = 8
HEAD_SIZE = 128
GROUP_ROWS = 8
QKV = 7168
CACHE_SLOTS = 8192
CAP = 2
TOTAL_ROWS = 32
N_GRP = 4


def routing_pair(key):
    group_keys = jax.random.split(key, N_GRP)
    orders = jax.vmap(lambda single: jax.random.permutation(single, GROUP_ROWS))(group_keys)
    assign_all = (orders % N_GRP).astype(jnp.int32).reshape(N_GRP * GROUP_ROWS)
    coins = jax.random.randint(jax.random.fold_in(key, 5), (N_GRP * GROUP_ROWS,), 0, 2, dtype=jnp.int32)
    chosen = jax.random.randint(jax.random.fold_in(key, 6), (), 0, N_GRP, dtype=jnp.int32)
    finish_all = jnp.where(assign_all == chosen, 1, coins).astype(jnp.int32)
    return (assign_all, finish_all)


def draw_assignment(key, part):
    assign_all, finish_all = routing_pair(key)
    return assign_all


def draw_finished(key, part):
    assign_all, finish_all = routing_pair(key)
    return finish_all


def draw_lengths(key, part):
    key = jax.random.fold_in(key, 17)
    drawn = jax.random.randint(key, (N_GRP * GROUP_ROWS,), 1, CACHE_SLOTS + 1, dtype=jnp.int32)
    longest = jax.random.randint(jax.random.fold_in(key, 1), (), 0, N_GRP * GROUP_ROWS, dtype=jnp.int32)
    return jnp.where(jnp.arange(N_GRP * GROUP_ROWS, dtype=jnp.int32) == longest, CACHE_SLOTS, drawn).astype(jnp.int32)


def lifted_keys(key, base_scale):
    total_rows = N_GRP * GROUP_ROWS
    width = KEY_VALUE_HEADS * HEAD_SIZE
    base = jnp.clip(jax.random.normal(key, (total_rows, CACHE_SLOTS, width), jnp.float32), -6.0, 6.0)
    strong = jnp.clip(jax.random.normal(jax.random.fold_in(key, 2), (total_rows, CACHE_SLOTS, width), jnp.float32), -2.25, 2.25) * 64.0
    picks = jax.random.randint(jax.random.fold_in(key, 1), (total_rows, CACHE_SLOTS, 1), 0, 16)
    row_index = jnp.arange(total_rows, dtype=jnp.int32)[:, None, None]
    chosen = (picks == 0) & (row_index % 4 == 0)
    return jnp.where(chosen, strong, base * base_scale)


def draw_key_cache(key, part):
    key = jax.random.fold_in(key, 11)
    values = lifted_keys(key, 2.5)
    return values.astype(jnp.bfloat16)


def level_of(stream_key, extent, shards, smallest, largest):
    factor_of = 1.0
    for axis_at, shards_of in shards:
        heights = jax.random.uniform(jax.random.fold_in(jax.random.fold_in(stream_key, 6), axis_at), (shards_of,), jnp.float32, smallest / len(shards), largest / len(shards))
        factor_of = factor_of * jnp.repeat(jnp.exp(heights), extent[axis_at] // shards_of).reshape((-1,) + (1,) * (len(extent) - 1 - axis_at))
    return factor_of


def centred(stream_key, shape, scale, bound, shards=(), kind=jnp.bfloat16):
    gain = level_of(stream_key, shape, shards, -0.22, 0.18) if shards else 1.0
    result = jax.random.normal(stream_key, shape, jnp.float32) * scale * gain
    return jnp.minimum(jnp.maximum(result, -bound), bound).astype(kind)


def setup_inputs(seed: int = 0) -> dict:
    key_list = jax.random.split(jax.random.key(seed), 9)
    hidden_in = centred(key_list[0], (TOTAL_ROWS, D), 1.0, 6.0, ((0, 4), (1, 64)))
    w_qkv = centred(key_list[1], (D, QKV), D ** -0.5, 0.078125, ((1, 256),))
    w_o = centred(key_list[2], (QUERY_HEADS * HEAD_SIZE, D), (QUERY_HEADS * HEAD_SIZE // 16) ** -0.5, 0.3125, ((1, 256),))
    key_cache = draw_key_cache(jax.random.fold_in(key_list[8], 71), 0)
    value_cache = centred(key_list[4], (TOTAL_ROWS, CACHE_SLOTS, KEY_VALUE_HEADS * HEAD_SIZE), 1.0, 6.0, ((0, 4), (1, 64)))
    lengths = draw_lengths(jax.random.fold_in(key_list[8], 71), 0)
    finished = draw_finished(jax.random.fold_in(key_list[8], 71), 0)
    assignment = draw_assignment(jax.random.fold_in(key_list[8], 71), 0)
    return dict(hidden_in=hidden_in, w_qkv=w_qkv, w_o=w_o, key_cache=key_cache, value_cache=value_cache, lengths=lengths, finished=finished, assignment=assignment)


NEG_FILL = -1e+30

def attend_row(items):
    query_vector, fresh_key, fresh_value, row_keys, row_values, length = items
    rows_per_group = QUERY_HEADS // KEY_VALUE_HEADS
    score_factor = 1.0 / math.sqrt(HEAD_SIZE)
    query_vector = query_vector.astype(jnp.float32).reshape(KEY_VALUE_HEADS, rows_per_group, HEAD_SIZE)
    row_keys = row_keys.astype(jnp.float32).reshape(CACHE_SLOTS, KEY_VALUE_HEADS, HEAD_SIZE)
    row_values = row_values.astype(jnp.float32).reshape(CACHE_SLOTS, KEY_VALUE_HEADS, HEAD_SIZE)
    scores = jnp.einsum('hgd,jhd->hgj', query_vector, row_keys) * score_factor
    is_valid = jnp.arange(CACHE_SLOTS, dtype=jnp.int32)[None, None, :] < length
    scores = jnp.where(is_valid, scores, NEG_FILL)
    self_score = jnp.einsum('pcv,pv->pc', query_vector, fresh_key.astype(jnp.float32).reshape(KEY_VALUE_HEADS, HEAD_SIZE)) * score_factor
    top_score = jnp.maximum(lax.optimization_barrier(jnp.max(scores, axis=-1)), self_score)
    weights = jnp.where(is_valid, jnp.exp(scores - top_score[..., None]), 0.0)
    self_weight = jnp.exp(self_score - top_score)
    denominator = lax.optimization_barrier(jnp.sum(weights, axis=-1)) + self_weight
    rounded = lax.optimization_barrier(weights.astype(jnp.bfloat16)).astype(jnp.float32)
    summed_output = jnp.einsum('hgj,jhd->hgd', rounded, row_values)
    summed_output = summed_output + self_weight[..., None] * fresh_value.astype(jnp.float32).reshape(KEY_VALUE_HEADS, 1, HEAD_SIZE)
    return (summed_output / denominator[..., None]).reshape(QUERY_HEADS * HEAD_SIZE)

def reference(hidden_in, w_qkv, w_o, key_cache, value_cache, lengths, finished, assignment):
    qkv = jnp.dot(hidden_in, w_qkv, preferred_element_type=jnp.float32).astype(jnp.bfloat16)
    query_width = QUERY_HEADS * HEAD_SIZE
    key_value_width = KEY_VALUE_HEADS * HEAD_SIZE
    query_rows = qkv[:, :query_width]
    fresh_keys = qkv[:, query_width:query_width + key_value_width]
    fresh_values = qkv[:, query_width + key_value_width:]
    attended = lax.map(attend_row, (query_rows, fresh_keys, fresh_values, key_cache, value_cache, lengths))
    attended = attended.astype(jnp.bfloat16)
    hidden_out = jnp.dot(attended, w_o, preferred_element_type=jnp.float32)
    assign_grid = assignment.reshape(N_GRP, GROUP_ROWS)
    finish_grid = finished.reshape(N_GRP, GROUP_ROWS)
    learners = jnp.arange(N_GRP, dtype=jnp.int32)
    matches = ((assign_grid[:, :, None] == learners[None, None, :]) & (finish_grid[:, :, None] == 1)).astype(jnp.int32)
    ranks = jnp.cumsum(matches, axis=1) - 1
    slots = jnp.arange(CAP, dtype=jnp.int32)
    table = (matches[:, None, None, :, :] == 1) & (ranks[:, None, None, :, :] == slots[None, None, :, None, None])
    table = jnp.transpose(table[:, 0], (0, 3, 1, 2)).astype(jnp.float32)
    outputs = hidden_out.reshape(N_GRP, GROUP_ROWS, D)
    returned = jnp.einsum('gacr,grd->agcd', table, outputs, precision=lax.Precision.HIGHEST).reshape(N_GRP * N_GRP * CAP, D)
    return (hidden_out, returned, w_qkv, w_o)
```

```python
import functools
import math

import jax
import jax.numpy as jnp
from jax import lax
from jax.experimental import pallas as pl
from jax.experimental.pallas import tpu as pltpu
from jax.sharding import Mesh
from jax.sharding import PartitionSpec as P

N_DEV = 64
N_GRP = 4
ROWS = 8
HEADS = 40
KV_HEADS = 8
SHARE = HEADS // KV_HEADS
LANES = 128
D = 5120
FEAT = D // N_DEV
WQ = 28
WO = 20
PIECE = 48
QW = N_DEV * WQ
OW = N_DEV * WO
POS = 128
NEG = -1e30

G_AXES = ("xh", "core")
D_AXES = ("xl", "y", "z")
F32 = jnp.float32
BF16 = jnp.bfloat16
VMEM = pl.BlockSpec(memory_space=pltpu.VMEM)
SMEM = pl.BlockSpec(memory_space=pltpu.SMEM)
PARAMS = pltpu.CompilerParams(vmem_limit_bytes=48 * 1024 * 1024)


def lane_iota(rows):
    return lax.broadcasted_iota(jnp.int32, (rows, LANES), 1)


def rolled(x, shift):
    shift %= LANES
    return x if shift == 0 else pltpu.roll(x, shift, 1)


def cut(tiles, start, width, lane):
    at, off = divmod(start, LANES)
    first = rolled(tiles[at], -off)
    if off + width <= LANES:
        return first
    return jnp.where(lane < LANES - off, first, rolled(tiles[at + 1], -off))


def lay(count, pieces, lane):
    tiles = [None] * count
    for source, first, width, column in pieces:
        moved = rolled(source, column - first)
        at, off = divmod(column, LANES)
        tiles[at] = moved if tiles[at] is None else jnp.where(lane >= off, moved, tiles[at])
        if off + width > LANES:
            tiles[at + 1] = moved
    return tiles


def swapped_blocks(blocks, group):
    odd = (group & 1) == 1
    high = (group & 2) == 2
    a, b, c, d = blocks
    a, b, c, d = (
        jnp.where(odd, b, a),
        jnp.where(odd, a, b),
        jnp.where(odd, d, c),
        jnp.where(odd, c, d),
    )
    return (
        jnp.where(high, c, a),
        jnp.where(high, d, b),
        jnp.where(high, a, c),
        jnp.where(high, b, d),
    )


def pack_kernel(hidden_ref, wq_ref, wo_ref, out_ref, rows_ref):
    lane = lane_iota(PIECE)
    rows_ref[0:WQ, :] = wq_ref[...].astype(F32)
    rows_ref[WQ:PIECE, :] = wo_ref[...].astype(F32)
    hidden = jnp.concatenate(
        [hidden_ref[...].astype(F32), jnp.zeros((ROWS, LANES - FEAT), F32)], axis=1
    )
    spare = jnp.concatenate(
        [
            pltpu.roll(hidden, FEAT, 1),
            pltpu.roll(hidden, 2 * FEAT - LANES, 1),
            jnp.zeros((PIECE - 2 * ROWS, LANES), F32),
        ],
        axis=0,
    )
    for dest in range(N_DEV):
        at, off = divmod(dest * FEAT, LANES)
        tiles = {at: rows_ref[:, at * LANES : (at + 1) * LANES]}
        if off + FEAT > LANES:
            tiles[at + 1] = rows_ref[:, (at + 1) * LANES : (at + 2) * LANES]
        piece = cut(tiles, dest * FEAT, FEAT, lane)
        piece = jnp.where(lane < FEAT, piece, spare)
        out_ref[dest * PIECE : (dest + 1) * PIECE, :] = piece.astype(BF16)


def project_kernel(group_ref, recv_ref, w0_ref, w1_ref, w2_ref, w3_ref, out_ref, w_ref):
    lane = lane_iota(ROWS)
    group = group_ref[0]
    for j, ref in enumerate((w0_ref, w1_ref, w2_ref, w3_ref)):
        w_ref[32 * j + 16 : 32 * j + 32, :] = jnp.zeros((16, D), BF16)
        w_ref[32 * j : 32 * j + WQ, :] = ref[...]
    pieces = []
    for dev in range(N_DEV):
        both = recv_ref[dev * PIECE : dev * PIECE + 16, :].astype(F32)
        pieces.append((both[0:8], FEAT, LANES - FEAT, dev * FEAT))
        pieces.append((both[8:16], FEAT, 2 * FEAT - LANES, dev * FEAT + LANES - FEAT))
    tiles = lay(D // LANES, pieces, lane)
    hidden = jnp.concatenate([t.astype(BF16) for t in tiles], axis=1)
    y = lax.dot_general(hidden, w_ref[...], (((1,), (1,)), ((), ())), preferred_element_type=F32)
    up, down = pltpu.roll(y, 32, 1), pltpu.roll(y, LANES - 32, 1)
    y = jnp.where((group & 1) == 1, jnp.where((lane & 32) == 0, down, up), y)
    y = jnp.where((group & 2) == 2, pltpu.roll(y, 64, 1), y)
    two = jnp.concatenate([y, y], axis=0).astype(BF16)
    for pair in range(N_DEV // 2):
        out_ref[16 * pair : 16 * pair + 16, :] = two


def turn_kernel(recv_ref, out_ref, q_ref, o_ref):
    for dev in range(N_DEV):
        x = recv_ref[dev * PIECE : (dev + 1) * PIECE, :].astype(F32)
        q_ref[dev * WQ : (dev + 1) * WQ, :] = x[0:WQ]
        o_ref[dev * WO : (dev + 1) * WO, :] = x[WQ:PIECE]
    row = lax.broadcasted_iota(jnp.int32, (FEAT, LANES), 0)
    eye = (row == lax.broadcasted_iota(jnp.int32, (FEAT, LANES), 1)).astype(BF16)
    turn = functools.partial(
        lax.dot_general,
        dimension_numbers=(((1,), (1,)), ((), ())),
        preferred_element_type=F32,
    )
    out_ref[:, 0:QW] = turn(eye, q_ref[...].astype(BF16)).astype(BF16)
    out_ref[:, QW : QW + OW] = turn(eye, o_ref[...].astype(BF16)).astype(BF16)


def attend_kernel(dev_ref, lengths_ref, recv_ref, keys_ref, values_ref, out_ref):
    lane = lane_iota(ROWS)
    sub = lax.broadcasted_iota(jnp.int32, (ROWS, LANES), 0)
    dev = dev_ref[0]
    scale = 1.0 / math.sqrt(LANES)
    offset = dev * POS
    sources = []
    for pair in range(N_DEV // 2):
        both = recv_ref[16 * pair : 16 * pair + 16, :].astype(F32)
        sources += [both[0:8], both[8:16]]
    pieces = [
        (sources[d], 32 * g, WQ, g * QW + d * WQ) for g in range(N_GRP) for d in range(N_DEV)
    ]
    tiles = lay(N_GRP * QW // LANES, pieces, lane)
    own_rows = [sub == r for r in range(ROWS)]
    length = jnp.zeros((ROWS, LANES), jnp.int32)
    for r in range(ROWS):
        length = jnp.where(own_rows[r], lengths_ref[r], length)
    valid = offset + lane < length
    valid = jnp.concatenate([valid] * SHARE, axis=0)
    first = dev == 0
    outs, tops, sums = [], [], []
    for k in range(KV_HEADS):
        heads = tiles[k * SHARE : (k + 1) * SHARE]
        new_key, new_value = tiles[HEADS + k], tiles[HEADS + KV_HEADS + k]
        q = jnp.concatenate(heads, axis=0)
        columns = slice(k * LANES, (k + 1) * LANES)
        keys = keys_ref[:, columns]
        wide = lax.dot_general(
            q.astype(BF16), keys, (((1,), (1,)), ((), ())), preferred_element_type=F32
        )
        s = []
        for i in range(SHARE):
            line = wide[i * ROWS : (i + 1) * ROWS, 0:LANES]
            for r in range(1, ROWS):
                line = jnp.where(
                    own_rows[r],
                    wide[i * ROWS : (i + 1) * ROWS, r * LANES : (r + 1) * LANES],
                    line,
                )
            s.append(line)
        s = jnp.concatenate(s, axis=0) * scale
        s = jnp.where(valid, s, NEG)
        own = jnp.sum(q * jnp.concatenate([new_key] * SHARE, axis=0), axis=1, keepdims=True) * scale
        own = jnp.where(first, own, NEG)
        top = jnp.maximum(jnp.max(s, axis=1, keepdims=True), own)
        w = jnp.where(valid, jnp.exp(s - top), 0.0)
        own_w = jnp.where(first, jnp.exp(own - top), 0.0)
        total = jnp.sum(w, axis=1, keepdims=True) + own_w
        spread = []
        for r in range(ROWS):
            spread.append(
                jnp.concatenate(
                    [
                        jnp.where(own_rows[r], w[i * ROWS : (i + 1) * ROWS], 0.0)
                        for i in range(SHARE)
                    ],
                    axis=0,
                ).astype(BF16)
            )
        spread = jnp.concatenate(spread, axis=1)
        out = jnp.dot(spread, values_ref[:, columns], preferred_element_type=F32)
        out = out + own_w * jnp.concatenate([new_value] * SHARE, axis=0)
        for i in range(SHARE):
            rows = slice(i * ROWS, (i + 1) * ROWS)
            outs.append(out[rows])
            tops.append(jnp.broadcast_to(top[rows], (ROWS, LANES)))
            sums.append(jnp.broadcast_to(total[rows], (ROWS, LANES)))
    for dest in range(N_DEV):
        h0, h1 = dest * FEAT // LANES, (dest * FEAT + FEAT - 1) // LANES
        tile = cut(outs, dest * FEAT, FEAT, lane)
        tile = jnp.where(lane < FEAT, tile, tops[h0])
        tile = jnp.where(lane == FEAT + 1, sums[h0], tile)
        tile = jnp.where(lane == FEAT + 2, tops[h1], tile)
        tile = jnp.where(lane == FEAT + 3, sums[h1], tile)
        out_ref[dest * ROWS : (dest + 1) * ROWS, :] = tile


def finish_kernel(place_ref, recv_ref, b0_ref, b1_ref, b2_ref, b3_ref, out_ref):
    lane = lane_iota(ROWS)
    dev, group = place_ref[0], place_ref[1]
    start = dev * FEAT
    split = ((start + FEAT - 1) // LANES) * LANES - start
    split = jnp.where(split <= 0, FEAT, split)
    left = (lane < split) | (lane == FEAT) | (lane == FEAT + 1)
    parts = [recv_ref[s * ROWS : (s + 1) * ROWS, :] for s in range(N_DEV)]
    tops = parts
    while len(tops) > 1:
        tops = [jnp.maximum(a, b) for a, b in zip(tops[0::2], tops[1::2])]
    top = tops[0]
    total = [jnp.zeros((ROWS, LANES), F32) for _ in range(4)]
    for s, part in enumerate(parts):
        e = jnp.exp(part - top)
        f = jnp.where(left, e[:, FEAT : FEAT + 1], e[:, FEAT + 2 : FEAT + 3])
        total[s % 4] = total[s % 4] + f * part
    total = (total[0] + total[1]) + (total[2] + total[3])
    den = jnp.where(left, total[:, FEAT + 1 : FEAT + 2], total[:, FEAT + 3 : FEAT + 4])
    attn = (total / den)[:, 0:FEAT].astype(BF16)
    blocks = [
        jnp.dot(attn, ref[:, QW : QW + OW], preferred_element_type=F32)
        for ref in (b0_ref, b1_ref, b2_ref, b3_ref)
    ]
    blocks = swapped_blocks(blocks, group)
    tiles = [
        block[:, t * LANES : (t + 1) * LANES] for block in blocks for t in range(OW // LANES)
    ]
    for dest in range(N_DEV):
        out_ref[dest * ROWS : (dest + 1) * ROWS, :] = cut(tiles, dest * FEAT, FEAT, lane)


def total_kernel(table_ref, recv_ref, hidden_ref, r0_ref, r1_ref, r2_ref, r3_ref):
    sums = [recv_ref[s * ROWS : (s + 1) * ROWS, :] for s in range(N_DEV)]
    while len(sums) > 1:
        sums = [a + b for a, b in zip(sums[0::2], sums[1::2])]
    hidden = sums[0]
    hidden_ref[...] = hidden[:, 0:FEAT]
    table = table_ref[...]
    packed = table[:, 0:1] * hidden[0:1, :]
    for r in range(1, ROWS):
        packed = packed + table[:, r : r + 1] * hidden[r : r + 1, :]
    for j, ref in enumerate((r0_ref, r1_ref, r2_ref, r3_ref)):
        ref[...] = packed[2 * j : 2 * j + 2, 0:FEAT]


def call(kernel, outs, scratch=(), smem=0, n_in=1):
    many = isinstance(outs, (list, tuple))
    return pl.pallas_call(
        kernel,
        out_shape=outs,
        in_specs=[SMEM] * smem + [VMEM] * (n_in - smem),
        out_specs=[VMEM] * len(outs) if many else VMEM,
        scratch_shapes=list(scratch),
        compiler_params=PARAMS,
    )


def to_groups(x):
    swap = [(0, 1), (1, 0)]
    return (
        lax.ppermute(x, "core", swap),
        lax.ppermute(x, "xh", swap),
        lax.ppermute(x, G_AXES, [(g, g ^ 3) for g in range(N_GRP)]),
    )


def exchange(x):
    rows = x.shape[0] // N_DEV
    x = x.reshape(N_DEV, rows, x.shape[1])
    x = lax.all_to_all(x, D_AXES, split_axis=0, concat_axis=0, tiled=True)
    return x.reshape(N_DEV * rows, x.shape[2])


def shards(hidden_in, w_qkv, w_o, key_cache, value_cache, lengths, finished, assignment):
    struct = jax.ShapeDtypeStruct
    group = lax.axis_index(G_AXES).astype(jnp.int32)
    dev = lax.axis_index(D_AXES).astype(jnp.int32)
    group_one, dev_one = group.reshape(1), dev.reshape(1)
    place = jnp.stack([dev, group])

    wq, wo = w_qkv.T, w_o.T
    others = to_groups(wq)
    sent = call(
        pack_kernel,
        struct((N_DEV * PIECE, LANES), BF16),
        [pltpu.VMEM((PIECE, D), F32)],
        n_in=3,
    )(hidden_in, wq, wo)
    recv = exchange(sent)
    sent = call(
        project_kernel,
        struct((N_DEV * ROWS, LANES), BF16),
        [pltpu.VMEM((LANES, D), BF16)],
        smem=1,
        n_in=6,
    )(group_one, recv, wq, *others)
    got = exchange(sent)

    block = call(
        turn_kernel,
        struct((FEAT, QW + OW), BF16),
        [pltpu.VMEM((QW, LANES), F32), pltpu.VMEM((OW, LANES), F32)],
    )(recv)
    blocks = (block,) + to_groups(block)

    sent = call(
        attend_kernel, struct((N_DEV * ROWS, LANES), F32), smem=2, n_in=5
    )(
        dev_one,
        lengths,
        got,
        key_cache.reshape(ROWS * POS, KV_HEADS * LANES),
        value_cache.reshape(ROWS * POS, KV_HEADS * LANES),
    )
    got = exchange(sent)
    sent = call(finish_kernel, struct((N_DEV * ROWS, LANES), F32), smem=1, n_in=6)(
        place, got, *blocks
    )
    got = exchange(sent)

    learners = jnp.arange(N_GRP, dtype=jnp.int32) ^ group
    matches = (assignment[None, :] == learners[:, None]) & (finished[None, :] == 1)
    ranks = jnp.cumsum(matches.astype(jnp.int32), axis=1)
    slots = jnp.arange(1, 3, dtype=jnp.int32)
    table = matches[:, None, :] & (ranks[:, None, :] == slots[None, :, None])
    table = table.reshape(ROWS, ROWS).astype(F32)
    part = struct((2, FEAT), F32)
    hidden_out, r0, r1, r2, r3 = call(
        total_kernel, [struct((ROWS, FEAT), F32)] + [part] * 4, n_in=2
    )(table, got)
    swap = [(0, 1), (1, 0)]
    r1 = lax.ppermute(r1, "core", swap)
    r2 = lax.ppermute(r2, "xh", swap)
    r3 = lax.ppermute(r3, G_AXES, [(g, g ^ 3) for g in range(N_GRP)])
    returned = jnp.concatenate(swapped_blocks((r0, r1, r2, r3), group), axis=0)

    ordered = swapped_blocks(blocks, group)
    w_qkv_gen = jnp.concatenate([b[:, 0:QW] for b in ordered], axis=1)
    w_o_gen = jnp.concatenate([b[:, QW:] for b in ordered], axis=1)
    return (hidden_out, returned, w_qkv_gen, w_o_gen)


def solution(mesh):
    fine = Mesh(mesh.devices.reshape(2, 2, 2, 4, 8), G_AXES + D_AXES)
    return jax.shard_map(
        shards,
        mesh=fine,
        in_specs=(
            P(G_AXES, D_AXES),
            P(None, G_AXES + D_AXES),
            P(None, G_AXES + D_AXES),
            P(G_AXES, D_AXES, None),
            P(G_AXES, D_AXES, None),
            P(G_AXES),
            P(G_AXES),
            P(G_AXES),
        ),
        out_specs=(P(G_AXES, D_AXES), P(G_AXES, D_AXES), P(D_AXES, None), P(D_AXES, None)),
        check_vma=False,
    )
```

```python
import functools
import math

import jax
import jax.numpy as jnp
from jax import lax
from jax.experimental import pallas as pl
from jax.experimental.pallas import tpu as pltpu
from jax.sharding import Mesh
from jax.sharding import PartitionSpec as P

N_DEV = 64
N_GRP = 4
ROWS = 8
HEADS = 40
KV_HEADS = 8
SHARE = HEADS // KV_HEADS
LANES = 128
D = 5120
FEAT = D // N_DEV
WQ = 28
WO = 20
FULL = WQ + WO
PIECE = 40
MAIN = PIECE - ROWS
QW = N_DEV * WQ
OW = N_DEV * WO
POS = 128
NEG = -1e30

G_AXES = ("xh", "core")
D_AXES = ("xl", "y", "z")
F32 = jnp.float32
BF16 = jnp.bfloat16
VMEM = pl.BlockSpec(memory_space=pltpu.VMEM)
SMEM = pl.BlockSpec(memory_space=pltpu.SMEM)
ANY = pl.BlockSpec(memory_space=pl.ANY)
MIB = 1024 * 1024


def lane_iota(rows):
    return lax.broadcasted_iota(jnp.int32, (rows, LANES), 1)


def turned(lane, shift):
    return lane if shift % LANES == 0 else (lane - shift) & (LANES - 1)


def cut(tiles, start, width, lane):
    at, off = divmod(start, LANES)
    if off + width <= LANES:
        return tiles[at]
    return jnp.where(lane >= off, tiles[at], tiles[at + 1])


def lay(count, sources, width, lane):
    tiles = [None] * count
    for i, source in enumerate(sources):
        at, off = divmod(i * width, LANES)
        tiles[at] = source if tiles[at] is None else jnp.where(lane >= off, source, tiles[at])
        if off + width > LANES:
            tiles[at + 1] = source
    return tiles


def shift_of(dev, width):
    return (dev * width) & (LANES - 1)


def turned_back(x, shift):
    return pltpu.roll(x, (LANES - shift) & (LANES - 1), 1)


def halves(ref):
    parts = []
    for row in range(0, ref.shape[0], 16):
        both = ref[row : row + 16, :].astype(F32)
        parts += [both[0:8], both[8:16]]
    return parts


def swapped_blocks(blocks, group):
    odd = (group & 1) == 1
    high = (group & 2) == 2
    a, b, c, d = blocks
    a, b, c, d = (
        jnp.where(odd, b, a),
        jnp.where(odd, a, b),
        jnp.where(odd, d, c),
        jnp.where(odd, c, d),
    )
    return (
        jnp.where(high, c, a),
        jnp.where(high, d, b),
        jnp.where(high, a, c),
        jnp.where(high, b, d),
    )


def pack_kernel(
    dev_ref, hidden_hbm, wq_hbm, wo_hbm, out_ref, hidden_ref, wq_ref, wo_ref, rows_ref, spare_ref, sems
):
    copies = [
        pltpu.make_async_copy(hidden_hbm, hidden_ref, sems.at[0]),
        pltpu.make_async_copy(wq_hbm, wq_ref, sems.at[1]),
        pltpu.make_async_copy(wo_hbm, wo_ref, sems.at[2]),
    ]
    for copy in copies:
        copy.start()
    lane = lane_iota(MAIN)
    copies[0].wait()
    hidden = jnp.concatenate(
        [hidden_ref[...].astype(F32), jnp.zeros((ROWS, LANES - FEAT), F32)], axis=1
    )
    hidden = pltpu.roll(hidden, shift_of(dev_ref[0], FEAT), 1)
    copies[1].wait()
    rows_ref[0:WQ, :] = wq_ref[...].astype(F32)
    copies[2].wait()
    rows_ref[WQ:FULL, :] = wo_ref[...].astype(F32)
    for t in range(D // LANES):
        columns = slice(t * LANES, (t + 1) * LANES)
        rest = rows_ref[MAIN:FULL, columns]
        spare_ref[0:16, columns] = pltpu.roll(rest, FEAT, 1)
        spare_ref[16:32, columns] = pltpu.roll(rest, 2 * FEAT - LANES, 1)
    half = lane[0:16]
    from_spare = jnp.concatenate([turned(half, FEAT), turned(half, 2 * FEAT - LANES)], axis=0)
    pair = []
    for dest in range(N_DEV):
        at, off = divmod(dest * FEAT, LANES)
        main = {t: rows_ref[0:MAIN, t * LANES : (t + 1) * LANES] for t in (at, at + 1) if t < D // LANES}
        spare = {t: spare_ref[:, t * LANES : (t + 1) * LANES] for t in (at, at + 1) if t < D // LANES}
        piece = jnp.where(
            turned(lane, off) < FEAT,
            cut(main, dest * FEAT, FEAT, lane),
            cut(spare, dest * FEAT, FEAT, from_spare),
        )
        pair += [hidden, piece]
        if dest % 2:
            out_ref[(dest - 1) * PIECE : (dest + 1) * PIECE, :] = jnp.concatenate(
                pair, axis=0
            ).astype(BF16)
            pair = []


def project_kernel(
    dev_ref, group_ref, recv_ref, own_hbm, w1_ref, w2_ref, w3_ref, out_ref, w_ref, own_ref, sem
):
    own = pltpu.make_async_copy(own_hbm, own_ref, sem)
    own.start()
    lane = lane_iota(ROWS)
    dev, group = dev_ref[0], group_ref[0]
    for j, ref in enumerate((own_ref, w1_ref, w2_ref, w3_ref)):
        if j == 0:
            continue
        w_ref[32 * j + 16 : 32 * j + 32, :] = jnp.zeros((16, D), BF16)
        w_ref[32 * j : 32 * j + WQ, :] = ref[...]
    sources = []
    for source in range(N_DEV):
        row = source * PIECE - source * PIECE % 16
        both = recv_ref[row : row + 16, :].astype(F32)
        sources.append(both[8:16] if source % 2 else both[0:8])
    tiles = lay(D // LANES, sources, FEAT, lane)
    hidden = jnp.concatenate([t.astype(BF16) for t in tiles], axis=1)
    own.wait()
    w_ref[16:32, :] = jnp.zeros((16, D), BF16)
    w_ref[0:WQ, :] = own_ref[...]
    y = lax.dot_general(hidden, w_ref[...], (((1,), (1,)), ((), ())), preferred_element_type=F32)
    up, down = pltpu.roll(y, 32, 1), pltpu.roll(y, LANES - 32, 1)
    y = jnp.where((group & 1) == 1, jnp.where((lane & 32) == 0, down, up), y)
    y = jnp.where((group & 2) == 2, pltpu.roll(y, 64, 1), y)
    y = pltpu.roll(y, shift_of(dev, WQ), 1)
    two = jnp.concatenate([y, y], axis=0).astype(BF16)
    for pair in range(N_DEV // 2):
        out_ref[16 * pair : 16 * pair + 16, :] = two


def turn(dev, x):
    row = lax.broadcasted_iota(jnp.int32, (FEAT, LANES), 0)
    eye = (((row + shift_of(dev, FEAT)) & (LANES - 1)) == lane_iota(FEAT)).astype(BF16)
    return lax.dot_general(
        eye, x.astype(BF16), (((1,), (1,)), ((), ())), preferred_element_type=F32
    ).astype(BF16)


def turn_o_kernel(dev_ref, recv_ref, after_ref, out_ref, rows_ref):
    shift = shift_of(dev_ref[0], FEAT)
    first = ((lane_iota(16) - shift) & (LANES - 1)) < LANES - FEAT
    for source in range(N_DEV):
        if source % 2 == 0:
            both = recv_ref[source * PIECE : (source + 2) * PIECE, :].astype(F32)
        piece = both[source % 2 * PIECE + ROWS : (source % 2 + 1) * PIECE]
        rest = jnp.where(
            first,
            pltpu.roll(piece[0:16], LANES - FEAT, 1),
            pltpu.roll(piece[16:32], 2 * LANES - 2 * FEAT, 1),
        )
        rows_ref[source * WO : source * WO + MAIN - WQ, :] = piece[WQ:MAIN]
        rows_ref[source * WO + MAIN - WQ : (source + 1) * WO, :] = rest
    out_ref[...] = turn(dev_ref[0], rows_ref[...])


def turn_q_kernel(dev_ref, recv_ref, after_ref, out_ref, rows_ref):
    for source in range(N_DEV):
        if source % 2 == 0:
            both = recv_ref[source * PIECE : (source + 2) * PIECE, :].astype(F32)
        piece = both[source % 2 * PIECE + ROWS : (source % 2 + 1) * PIECE]
        rows_ref[source * WQ : (source + 1) * WQ, :] = piece[0:WQ]
    out_ref[...] = turn(dev_ref[0], rows_ref[...])


def attend_kernel(
    dev_ref, lengths_ref, recv_ref, keys_hbm, values_hbm, out_ref, keys_ref, values_ref, sems
):
    copies = []
    for i, (source, target) in enumerate(((keys_hbm, keys_ref), (values_hbm, values_ref))):
        for r in range(ROWS):
            rows = pl.ds(r * POS, POS)
            copies.append(
                pltpu.make_async_copy(source.at[rows], target.at[rows], sems.at[i, r])
            )
    for copy in copies:
        copy.start()
    lane = lane_iota(ROWS)
    sub = lax.broadcasted_iota(jnp.int32, (ROWS, LANES), 0)
    dev = dev_ref[0]
    scale = 1.0 / math.sqrt(LANES)
    sources = halves(recv_ref)
    tiles = []
    for g in range(N_GRP):
        frame = lay(QW // LANES, sources, WQ, turned(lane, 32 * g))
        tiles += [pltpu.roll(t, LANES - 32 * g, 1) for t in frame] if g else frame
    own_rows = [sub == r for r in range(ROWS)]
    valid = dev * POS + lane < lengths_ref[...]
    valid = jnp.concatenate([valid] * SHARE, axis=0)
    first = dev == 0

    for copy in copies[:ROWS]:
        copy.wait()
    weights = []
    for k in range(KV_HEADS):
        new_key = tiles[HEADS + k]
        q = jnp.concatenate(tiles[k * SHARE : (k + 1) * SHARE], axis=0)
        keys = keys_ref[:, k * LANES : (k + 1) * LANES]
        wide = lax.dot_general(
            q.astype(BF16), keys, (((1,), (1,)), ((), ())), preferred_element_type=F32
        )
        s = []
        for i in range(SHARE):
            line = wide[i * ROWS : (i + 1) * ROWS, 0:LANES]
            for r in range(1, ROWS):
                line = jnp.where(
                    own_rows[r],
                    wide[i * ROWS : (i + 1) * ROWS, r * LANES : (r + 1) * LANES],
                    line,
                )
            s.append(line)
        s = jnp.concatenate(s, axis=0) * scale
        s = jnp.where(valid, s, NEG)
        own = jnp.sum(q * jnp.concatenate([new_key] * SHARE, axis=0), axis=1, keepdims=True) * scale
        own = jnp.where(first, own, NEG)
        top = jnp.maximum(jnp.max(s, axis=1, keepdims=True), own)
        w = jnp.where(valid, jnp.exp(s - top), 0.0)
        own_w = jnp.where(first, jnp.exp(own - top), 0.0)
        weights.append((w, own_w, top, jnp.sum(w, axis=1, keepdims=True) + own_w))

    for copy in copies[ROWS:]:
        copy.wait()
    outs, tags = [], []
    at = lane & 7
    for k in range(KV_HEADS):
        w, own_w, top, total = weights[k]
        spread = []
        for r in range(ROWS):
            spread.append(
                jnp.concatenate(
                    [
                        jnp.where(own_rows[r], w[i * ROWS : (i + 1) * ROWS], 0.0)
                        for i in range(SHARE)
                    ],
                    axis=0,
                ).astype(BF16)
            )
        spread = jnp.concatenate(spread, axis=1)
        values = values_ref[:, k * LANES : (k + 1) * LANES]
        out = jnp.dot(spread, values, preferred_element_type=F32)
        out = out + own_w * jnp.concatenate([tiles[HEADS + KV_HEADS + k]] * SHARE, axis=0)
        for i in range(SHARE):
            rows = slice(i * ROWS, (i + 1) * ROWS)
            outs.append(out[rows])
            t = jnp.broadcast_to(top[rows], (ROWS, LANES))
            t0 = t.astype(BF16).astype(F32)
            t1 = (t - t0).astype(BF16).astype(F32)
            d = jnp.broadcast_to(total[rows], (ROWS, LANES))
            d0 = d.astype(BF16).astype(F32)
            tag = jnp.where(at == 0, t0, jnp.where(at == 1, t1, (t - t0) - t1))
            tags.append(jnp.where(at < 3, tag, jnp.where(at == 3, d0, d - d0)))
    pair = []
    for dest in range(N_DEV):
        h0, h1 = dest * FEAT // LANES, (dest * FEAT + FEAT - 1) // LANES
        tile = cut(outs, dest * FEAT, FEAT, lane)
        place = turned(lane, dest * FEAT)
        tile = jnp.where(place < FEAT, tile, jnp.where(place < FEAT + 8, tags[h0], tags[h1]))
        pair.append(tile)
        if dest % 2:
            out_ref[(dest - 1) * ROWS : (dest + 1) * ROWS, :] = jnp.concatenate(
                pair, axis=0
            ).astype(BF16)
            pair = []


def finish_kernel(dev_ref, group_ref, recv_ref, b0_ref, b1_ref, b2_ref, b3_ref, out_ref):
    lane = lane_iota(ROWS)
    dev, group = dev_ref[0], group_ref[0]
    start = dev * FEAT
    split = ((start + FEAT - 1) // LANES) * LANES - start
    split = jnp.where(split <= 0, FEAT, split)
    left = (lane < split) | ((lane >= FEAT) & (lane < FEAT + 8))
    shift = shift_of(dev, FEAT)
    parts = [turned_back(x, shift) for x in halves(recv_ref)]
    terms = [(x + pltpu.roll(x, LANES - 1, 1)) + pltpu.roll(x, LANES - 2, 1) for x in parts]
    tops = terms
    while len(tops) > 1:
        tops = [jnp.maximum(a, b) for a, b in zip(tops[0::2], tops[1::2])]
    top = tops[0]
    total = [jnp.zeros((ROWS, LANES), F32) for _ in range(4)]
    for s, part in enumerate(parts):
        e = jnp.exp(terms[s] - top)
        f = jnp.where(left, e[:, FEAT : FEAT + 1], e[:, FEAT + 8 : FEAT + 9])
        total[s % 4] = total[s % 4] + f * part
    total = (total[0] + total[1]) + (total[2] + total[3])
    den = total + pltpu.roll(total, LANES - 1, 1)
    den = jnp.where(left, den[:, FEAT + 3 : FEAT + 4], den[:, FEAT + 11 : FEAT + 12])
    attn = (total / den)[:, 0:FEAT].astype(BF16)
    blocks = [
        jnp.dot(attn, ref[...], preferred_element_type=F32)
        for ref in (b0_ref, b1_ref, b2_ref, b3_ref)
    ]
    blocks = swapped_blocks(blocks, group)
    tiles = [
        block[:, t * LANES : (t + 1) * LANES] for block in blocks for t in range(OW // LANES)
    ]
    for dest in range(0, N_DEV, 2):
        pair = [cut(tiles, d * FEAT, FEAT, lane) for d in (dest, dest + 1)]
        out_ref[dest * ROWS : (dest + 2) * ROWS, :] = jnp.concatenate(pair, axis=0).astype(BF16)


def total_kernel(dev_ref, table_ref, recv_ref, after_ref, hidden_ref, r0_ref, r1_ref, r2_ref, r3_ref):
    sums = halves(recv_ref)
    while len(sums) > 1:
        sums = [a + b for a, b in zip(sums[0::2], sums[1::2])]
    hidden = turned_back(sums[0], shift_of(dev_ref[0], FEAT))
    hidden_ref[...] = hidden[:, 0:FEAT]
    table = table_ref[...]
    packed = table[:, 0:1] * hidden[0:1, :]
    for r in range(1, ROWS):
        packed = packed + table[:, r : r + 1] * hidden[r : r + 1, :]
    for j, ref in enumerate((r0_ref, r1_ref, r2_ref, r3_ref)):
        ref[...] = packed[2 * j : 2 * j + 2, 0:FEAT]


def order_kernel(group_ref, after_ref, *refs):
    q_out, o_out, mark_ref = refs[8:]
    mark_ref[...] = jnp.zeros_like(mark_ref)
    for j in range(N_GRP):
        group = group_ref[0] ^ j
        q_out[:, pl.ds(pl.multiple_of(group * QW, LANES), QW)] = refs[j][...]
        o_out[:, pl.ds(pl.multiple_of(group * OW, LANES), OW)] = refs[N_GRP + j][...]


def call(kernel, outs, specs, scratch=(), vmem=32, flops=None):
    many = isinstance(outs, (list, tuple))
    return pl.pallas_call(
        kernel,
        out_shape=outs,
        in_specs=specs,
        out_specs=[VMEM] * len(outs) if many else VMEM,
        scratch_shapes=list(scratch),
        compiler_params=pltpu.CompilerParams(vmem_limit_bytes=vmem * MIB),
        cost_estimate=flops
        and pl.CostEstimate(flops=flops, bytes_accessed=4 * MIB, transcendentals=0),
    )


SWAP = [(0, 1), (1, 0)]


def to_groups(x):
    far = lax.ppermute(x, "xh", SWAP)
    return lax.ppermute(x, "core", SWAP), far, lax.ppermute(far, "core", SWAP)


def to_groups_at_once(x):
    return (
        lax.ppermute(x, "core", SWAP),
        lax.ppermute(x, "xh", SWAP),
        lax.ppermute(x, G_AXES, [(g, g ^ 3) for g in range(N_GRP)]),
    )


def exchange(x):
    rows = x.shape[0] // N_DEV
    x = x.reshape(N_DEV, rows, x.shape[1])
    x = lax.all_to_all(x, D_AXES, split_axis=0, concat_axis=0, tiled=True)
    return x.reshape(N_DEV * rows, x.shape[2])


def shards(hidden_in, w_qkv, w_o, key_cache, value_cache, lengths, finished, assignment):
    struct = jax.ShapeDtypeStruct
    group = lax.axis_index(G_AXES).astype(jnp.int32)
    dev = lax.axis_index(D_AXES).astype(jnp.int32)
    dev, group_one = dev.reshape(1), group.reshape(1)
    lengths = jnp.broadcast_to(lengths[:, None], (ROWS, LANES))

    wq, wo = w_qkv.T, w_o.T
    others = to_groups(wq)
    part = struct((N_DEV * ROWS, LANES), BF16)
    sent = call(
        pack_kernel,
        struct((N_DEV * PIECE, LANES), BF16),
        [SMEM] + [ANY] * 3,
        [
            pltpu.VMEM((ROWS, FEAT), BF16),
            pltpu.VMEM((WQ, D), BF16),
            pltpu.VMEM((WO, D), BF16),
            pltpu.VMEM((FULL, D), F32),
            pltpu.VMEM((MAIN, D), F32),
            pltpu.SemaphoreType.DMA((3,)),
        ],
        vmem=60,
    )(dev, hidden_in, wq, wo)
    recv = exchange(sent)
    sent = call(
        project_kernel,
        part,
        [SMEM, SMEM, VMEM, ANY] + [VMEM] * 3,
        [
            pltpu.VMEM((LANES, D), BF16),
            pltpu.VMEM((WQ, D), BF16),
            pltpu.SemaphoreType.DMA,
        ],
    )(dev, group_one, recv, wq, *others)
    got = exchange(sent)

    o_block = call(
        turn_o_kernel,
        struct((FEAT, OW), BF16),
        [SMEM, VMEM, ANY],
        [pltpu.VMEM((OW, LANES), F32)],
    )(dev, recv, sent)
    o_blocks = (o_block,) + to_groups(o_block)

    q_block = call(
        turn_q_kernel,
        struct((FEAT, QW), BF16),
        [SMEM, VMEM, ANY],
        [pltpu.VMEM((QW, LANES), F32)],
    )(dev, recv, sent)
    q_blocks = (q_block,) + to_groups(q_block)
    cache = (ROWS * POS, KV_HEADS * LANES)
    sent = call(
        attend_kernel,
        part,
        [SMEM, VMEM, VMEM, ANY, ANY],
        [pltpu.VMEM(cache, BF16)] * 2 + [pltpu.SemaphoreType.DMA((2, ROWS))],
        vmem=54,
        flops=10**11,
    )(dev, lengths, got, key_cache.reshape(cache), value_cache.reshape(cache))
    got = exchange(sent)
    sent = call(finish_kernel, part, [SMEM, SMEM] + [VMEM] * 5)(
        dev, group_one, got, *o_blocks
    )
    w_qkv_gen, w_o_gen, mark = call(
        order_kernel,
        [
            struct((FEAT, N_GRP * QW), BF16),
            struct((FEAT, N_GRP * OW), BF16),
            struct((ROWS, LANES), F32),
        ],
        [SMEM, ANY] + [VMEM] * 8,
    )(group_one, sent, *q_blocks, *o_blocks)
    got = exchange(sent)

    learners = jnp.arange(N_GRP, dtype=jnp.int32) ^ group
    matches = (assignment[None, :] == learners[:, None]) & (finished[None, :] == 1)
    ranks = jnp.cumsum(matches.astype(jnp.int32), axis=1)
    slots = jnp.arange(1, 3, dtype=jnp.int32)
    table = matches[:, None, :] & (ranks[:, None, :] == slots[None, :, None])
    table = table.reshape(ROWS, ROWS).astype(F32)
    few = struct((2, FEAT), F32)
    hidden_out, r0, r1, r2, r3 = call(
        total_kernel, [struct((ROWS, FEAT), F32)] + [few] * 4, [SMEM, VMEM, VMEM, ANY]
    )(dev, table, got, mark)
    r1 = lax.ppermute(r1, "core", SWAP)
    r2 = lax.ppermute(r2, "xh", SWAP)
    r3 = lax.ppermute(r3, G_AXES, [(g, g ^ 3) for g in range(N_GRP)])
    returned = jnp.concatenate(swapped_blocks((r0, r1, r2, r3), group), axis=0)
    return (hidden_out, returned, w_qkv_gen, w_o_gen)


def solution(mesh):
    fine = Mesh(mesh.devices.reshape(2, 2, 2, 4, 8), G_AXES + D_AXES)
    return jax.shard_map(
        shards,
        mesh=fine,
        in_specs=(
            P(G_AXES, D_AXES),
            P(None, G_AXES + D_AXES),
            P(None, G_AXES + D_AXES),
            P(G_AXES, D_AXES, None),
            P(G_AXES, D_AXES, None),
            P(G_AXES),
            P(G_AXES),
            P(G_AXES),
        ),
        out_specs=(P(G_AXES, D_AXES), P(G_AXES, D_AXES), P(D_AXES, None), P(D_AXES, None)),
        check_vma=False,
    )
```

```python
import functools
import math

import jax
import jax.numpy as jnp
from jax import lax
from jax.experimental import pallas as pl
from jax.experimental.pallas import tpu as pltpu
from jax.sharding import Mesh
from jax.sharding import PartitionSpec as P

N_DEV = 64
N_GRP = 4
ROWS = 8
HEADS = 40
KV_HEADS = 8
SHARE = HEADS // KV_HEADS
LANES = 128
D = 5120
FEAT = D // N_DEV
WQ = 28
WO = 20
FULL = WQ + WO
PIECE = 40
MAIN = PIECE - ROWS
QW = N_DEV * WQ
OW = N_DEV * WO
GROUP = ROWS * SHARE
POS = 128
NEG = -1e30

G_AXES = ("xh", "core")
D_AXES = ("xl", "y", "z")
F32 = jnp.float32
BF16 = jnp.bfloat16
VMEM = pl.BlockSpec(memory_space=pltpu.VMEM)
SMEM = pl.BlockSpec(memory_space=pltpu.SMEM)
ANY = pl.BlockSpec(memory_space=pl.ANY)
MIB = 1024 * 1024


def lane_iota(rows):
    return lax.broadcasted_iota(jnp.int32, (rows, LANES), 1)


def turned(lane, shift):
    return lane if shift % LANES == 0 else (lane - shift) & (LANES - 1)


def cut(tiles, start, width, lane):
    at, off = divmod(start, LANES)
    if off + width <= LANES:
        return tiles[at]
    return jnp.where(lane >= off, tiles[at], tiles[at + 1])


def lay(count, sources, width, lane):
    tiles = [None] * count
    for i, source in enumerate(sources):
        at, off = divmod(i * width, LANES)
        tiles[at] = source if tiles[at] is None else jnp.where(lane >= off, source, tiles[at])
        if off + width > LANES:
            tiles[at + 1] = source
    return tiles


def shift_of(dev, width):
    return (dev * width) & (LANES - 1)


def turned_back(x, shift):
    return pltpu.roll(x, (LANES - shift) & (LANES - 1), 1)


def halves(ref):
    parts = []
    for row in range(0, ref.shape[0], 16):
        both = ref[row : row + 16, :].astype(F32)
        parts += [both[0:8], both[8:16]]
    return parts


def swapped_blocks(blocks, group):
    odd = (group & 1) == 1
    high = (group & 2) == 2
    a, b, c, d = blocks
    a, b, c, d = (
        jnp.where(odd, b, a),
        jnp.where(odd, a, b),
        jnp.where(odd, d, c),
        jnp.where(odd, c, d),
    )
    return (
        jnp.where(high, c, a),
        jnp.where(high, d, b),
        jnp.where(high, a, c),
        jnp.where(high, b, d),
    )


def pack_kernel(
    dev_ref, hidden_hbm, wq_hbm, wo_hbm, out_ref, hidden_ref, wq_ref, wo_ref, rows_ref, spare_ref, sems
):
    copies = [
        pltpu.make_async_copy(hidden_hbm, hidden_ref, sems.at[0]),
        pltpu.make_async_copy(wq_hbm, wq_ref, sems.at[1]),
        pltpu.make_async_copy(wo_hbm, wo_ref, sems.at[2]),
    ]
    for copy in copies:
        copy.start()
    lane = lane_iota(MAIN)
    copies[0].wait()
    hidden = jnp.concatenate(
        [hidden_ref[...].astype(F32), jnp.zeros((ROWS, LANES - FEAT), F32)], axis=1
    )
    hidden = pltpu.roll(hidden, shift_of(dev_ref[0], FEAT), 1)
    copies[1].wait()
    rows_ref[0:WQ, :] = wq_ref[...].astype(F32)
    copies[2].wait()
    rows_ref[WQ:FULL, :] = wo_ref[...].astype(F32)
    for t in range(D // LANES):
        columns = slice(t * LANES, (t + 1) * LANES)
        rest = rows_ref[MAIN:FULL, columns]
        spare_ref[0:16, columns] = pltpu.roll(rest, FEAT, 1)
        spare_ref[16:32, columns] = pltpu.roll(rest, 2 * FEAT - LANES, 1)
    half = lane[0:16]
    from_spare = jnp.concatenate([turned(half, FEAT), turned(half, 2 * FEAT - LANES)], axis=0)
    pair = []
    for dest in range(N_DEV):
        at, off = divmod(dest * FEAT, LANES)
        main = {t: rows_ref[0:MAIN, t * LANES : (t + 1) * LANES] for t in (at, at + 1) if t < D // LANES}
        spare = {t: spare_ref[:, t * LANES : (t + 1) * LANES] for t in (at, at + 1) if t < D // LANES}
        piece = jnp.where(
            turned(lane, off) < FEAT,
            cut(main, dest * FEAT, FEAT, lane),
            cut(spare, dest * FEAT, FEAT, from_spare),
        )
        pair += [hidden, piece]
        if dest % 2:
            out_ref[(dest - 1) * PIECE : (dest + 1) * PIECE, :] = jnp.concatenate(
                pair, axis=0
            ).astype(BF16)
            pair = []


def project_kernel(
    dev_ref, group_ref, recv_ref, own_hbm, w2_ref, both_ref, out_ref, w_ref, own_ref, sem
):
    own = pltpu.make_async_copy(own_hbm, own_ref, sem)
    own.start()
    lane = lane_iota(ROWS)
    dev, group = dev_ref[0], group_ref[0]
    for j, ref in enumerate((own_ref, both_ref.at[0], w2_ref, both_ref.at[1])):
        if j == 0:
            continue
        w_ref[32 * j + 16 : 32 * j + 32, :] = jnp.zeros((16, D), BF16)
        w_ref[32 * j : 32 * j + WQ, :] = ref[...]
    sources = []
    for source in range(N_DEV):
        row = source * PIECE - source * PIECE % 16
        both = recv_ref[row : row + 16, :].astype(F32)
        sources.append(both[8:16] if source % 2 else both[0:8])
    tiles = lay(D // LANES, sources, FEAT, lane)
    hidden = jnp.concatenate([t.astype(BF16) for t in tiles], axis=1)
    own.wait()
    w_ref[16:32, :] = jnp.zeros((16, D), BF16)
    w_ref[0:WQ, :] = own_ref[...]
    y = lax.dot_general(hidden, w_ref[...], (((1,), (1,)), ((), ())), preferred_element_type=F32)
    up, down = pltpu.roll(y, 32, 1), pltpu.roll(y, LANES - 32, 1)
    y = jnp.where((group & 1) == 1, jnp.where((lane & 32) == 0, down, up), y)
    y = jnp.where((group & 2) == 2, pltpu.roll(y, 64, 1), y)
    y = pltpu.roll(y, shift_of(dev, WQ), 1)
    two = jnp.concatenate([y, y], axis=0).astype(BF16)
    for pair in range(N_DEV // 2):
        out_ref[16 * pair : 16 * pair + 16, :] = two


def turn(dev, x):
    row = lax.broadcasted_iota(jnp.int32, (FEAT, LANES), 0)
    eye = (((row + shift_of(dev, FEAT)) & (LANES - 1)) == lane_iota(FEAT)).astype(BF16)
    return lax.dot_general(
        eye, x.astype(BF16), (((1,), (1,)), ((), ())), preferred_element_type=F32
    ).astype(BF16)


def turn_o_kernel(dev_ref, lengths_ref, recv_ref, after_ref, out_ref, wide_ref, rows_ref):
    for r in range(ROWS):
        wide_ref[r : r + 1, :] = jnp.full((1, LANES), lengths_ref[r], jnp.int32)
    shift = shift_of(dev_ref[0], FEAT)
    first = ((lane_iota(16) - shift) & (LANES - 1)) < LANES - FEAT
    for source in range(N_DEV):
        if source % 2 == 0:
            both = recv_ref[source * PIECE : (source + 2) * PIECE, :].astype(F32)
        piece = both[source % 2 * PIECE + ROWS : (source % 2 + 1) * PIECE]
        rest = jnp.where(
            first,
            pltpu.roll(piece[0:16], LANES - FEAT, 1),
            pltpu.roll(piece[16:32], 2 * LANES - 2 * FEAT, 1),
        )
        rows_ref[source * WO : source * WO + MAIN - WQ, :] = piece[WQ:MAIN]
        rows_ref[source * WO + MAIN - WQ : (source + 1) * WO, :] = rest
    out_ref[...] = turn(dev_ref[0], rows_ref[...])


def turn_q_kernel(dev_ref, recv_ref, after_ref, out_ref, rows_ref):
    for source in range(N_DEV):
        if source % 2 == 0:
            both = recv_ref[source * PIECE : (source + 2) * PIECE, :].astype(F32)
        piece = both[source % 2 * PIECE + ROWS : (source % 2 + 1) * PIECE]
        rows_ref[source * WQ : (source + 1) * WQ, :] = piece[0:WQ]
    out_ref[...] = turn(dev_ref[0], rows_ref[...])


def score_kernel(dev_ref, lengths_ref, recv_ref, keys_ref, w_ref, own_ref, tag_ref, fresh_ref):
    lane = lane_iota(ROWS)
    sub = lax.broadcasted_iota(jnp.int32, (ROWS, LANES), 0)
    dev = dev_ref[0]
    scale = 1.0 / math.sqrt(LANES)
    sources = halves(recv_ref)
    tiles = []
    for g in range(N_GRP):
        frame = lay(QW // LANES, sources, WQ, turned(lane, 32 * g))
        tiles += [pltpu.roll(t, LANES - 32 * g, 1) for t in frame] if g else frame
    own_rows = [sub == r for r in range(ROWS)]
    valid = dev * POS + lane < lengths_ref[...]
    valid = jnp.concatenate([valid] * SHARE, axis=0)
    first = dev == 0
    at = lane_iota(GROUP) & 7
    for k in range(KV_HEADS):
        new_key = tiles[HEADS + k]
        q = jnp.concatenate(tiles[k * SHARE : (k + 1) * SHARE], axis=0)
        keys = keys_ref[:, k * LANES : (k + 1) * LANES]
        wide = lax.dot_general(
            q.astype(BF16), keys, (((1,), (1,)), ((), ())), preferred_element_type=F32
        )
        s = []
        for i in range(SHARE):
            line = wide[i * ROWS : (i + 1) * ROWS, 0:LANES]
            for r in range(1, ROWS):
                line = jnp.where(
                    own_rows[r],
                    wide[i * ROWS : (i + 1) * ROWS, r * LANES : (r + 1) * LANES],
                    line,
                )
            s.append(line)
        s = jnp.concatenate(s, axis=0) * scale
        s = jnp.where(valid, s, NEG)
        own = jnp.sum(q * jnp.concatenate([new_key] * SHARE, axis=0), axis=1, keepdims=True) * scale
        own = jnp.where(first, own, NEG)
        top = jnp.maximum(jnp.max(s, axis=1, keepdims=True), own)
        w = jnp.where(valid, jnp.exp(s - top), 0.0)
        own_w = jnp.where(first, jnp.exp(own - top), 0.0)
        total = jnp.sum(w, axis=1, keepdims=True) + own_w
        rows = slice(k * GROUP, (k + 1) * GROUP)
        w_ref[rows, :] = w
        own_ref[rows, :] = jnp.broadcast_to(own_w, (GROUP, LANES))
        t = jnp.broadcast_to(top, (GROUP, LANES))
        t0 = t.astype(BF16).astype(F32)
        t1 = (t - t0).astype(BF16).astype(F32)
        d = jnp.broadcast_to(total, (GROUP, LANES))
        d0 = d.astype(BF16).astype(F32)
        tag = jnp.where(at == 0, t0, jnp.where(at == 1, t1, (t - t0) - t1))
        tag_ref[rows, :] = jnp.where(at < 3, tag, jnp.where(at == 3, d0, d - d0))
        fresh_ref[k * ROWS : (k + 1) * ROWS, :] = tiles[HEADS + KV_HEADS + k]


def value_kernel(w_ref, own_ref, tag_ref, fresh_ref, values_ref, out_ref):
    lane = lane_iota(ROWS)
    sub = lax.broadcasted_iota(jnp.int32, (ROWS, LANES), 0)
    own_rows = [sub == r for r in range(ROWS)]
    outs, tags = [], []
    for k in range(KV_HEADS):
        heads = [slice(k * GROUP + i * ROWS, k * GROUP + (i + 1) * ROWS) for i in range(SHARE)]
        spread = []
        for r in range(ROWS):
            spread.append(
                jnp.concatenate(
                    [jnp.where(own_rows[r], w_ref[h, :], 0.0) for h in heads], axis=0
                ).astype(BF16)
            )
        spread = jnp.concatenate(spread, axis=1)
        values = values_ref[:, k * LANES : (k + 1) * LANES]
        out = jnp.dot(spread, values, preferred_element_type=F32)
        fresh = fresh_ref[k * ROWS : (k + 1) * ROWS, :]
        for i, h in enumerate(heads):
            outs.append(out[i * ROWS : (i + 1) * ROWS] + own_ref[h, :] * fresh)
            tags.append(tag_ref[h, :])
    pair = []
    for dest in range(N_DEV):
        h0, h1 = dest * FEAT // LANES, (dest * FEAT + FEAT - 1) // LANES
        tile = cut(outs, dest * FEAT, FEAT, lane)
        place = turned(lane, dest * FEAT)
        tile = jnp.where(place < FEAT, tile, jnp.where(place < FEAT + 8, tags[h0], tags[h1]))
        pair.append(tile)
        if dest % 2:
            out_ref[(dest - 1) * ROWS : (dest + 1) * ROWS, :] = jnp.concatenate(
                pair, axis=0
            ).astype(BF16)
            pair = []


def finish_kernel(dev_ref, group_ref, recv_ref, b0_ref, b1_ref, b2_ref, b3_ref, out_ref):
    lane = lane_iota(ROWS)
    dev, group = dev_ref[0], group_ref[0]
    start = dev * FEAT
    split = ((start + FEAT - 1) // LANES) * LANES - start
    split = jnp.where(split <= 0, FEAT, split)
    left = (lane < split) | ((lane >= FEAT) & (lane < FEAT + 8))
    shift = shift_of(dev, FEAT)
    parts = [turned_back(x, shift) for x in halves(recv_ref)]
    terms = [(x + pltpu.roll(x, LANES - 1, 1)) + pltpu.roll(x, LANES - 2, 1) for x in parts]
    tops = terms
    while len(tops) > 1:
        tops = [jnp.maximum(a, b) for a, b in zip(tops[0::2], tops[1::2])]
    top = tops[0]
    total = [jnp.zeros((ROWS, LANES), F32) for _ in range(4)]
    for s, part in enumerate(parts):
        e = jnp.exp(terms[s] - top)
        f = jnp.where(left, e[:, FEAT : FEAT + 1], e[:, FEAT + 8 : FEAT + 9])
        total[s % 4] = total[s % 4] + f * part
    total = (total[0] + total[1]) + (total[2] + total[3])
    den = total + pltpu.roll(total, LANES - 1, 1)
    den = jnp.where(left, den[:, FEAT + 3 : FEAT + 4], den[:, FEAT + 11 : FEAT + 12])
    attn = (total / den)[:, 0:FEAT].astype(BF16)
    blocks = [
        jnp.dot(attn, ref[...], preferred_element_type=F32)
        for ref in (b0_ref, b1_ref, b2_ref, b3_ref)
    ]
    blocks = swapped_blocks(blocks, group)
    tiles = [
        block[:, t * LANES : (t + 1) * LANES] for block in blocks for t in range(OW // LANES)
    ]
    for dest in range(0, N_DEV, 2):
        pair = [cut(tiles, d * FEAT, FEAT, lane) for d in (dest, dest + 1)]
        out_ref[dest * ROWS : (dest + 2) * ROWS, :] = jnp.concatenate(pair, axis=0).astype(BF16)


def total_kernel(dev_ref, table_ref, recv_ref, after_ref, hidden_ref, r0_ref, r1_ref, r2_ref, r3_ref):
    sums = halves(recv_ref)
    while len(sums) > 1:
        sums = [a + b for a, b in zip(sums[0::2], sums[1::2])]
    hidden = turned_back(sums[0], shift_of(dev_ref[0], FEAT))
    hidden_ref[...] = hidden[:, 0:FEAT]
    table = table_ref[...]
    packed = table[:, 0:1] * hidden[0:1, :]
    for r in range(1, ROWS):
        packed = packed + table[:, r : r + 1] * hidden[r : r + 1, :]
    for j, ref in enumerate((r0_ref, r1_ref, r2_ref, r3_ref)):
        ref[...] = packed[2 * j : 2 * j + 2, 0:FEAT]


def order_kernel(group_ref, after_ref, *refs):
    q_out, o_out, mark_ref = refs[8:]
    mark_ref[...] = jnp.zeros_like(mark_ref)
    for j in range(N_GRP):
        group = group_ref[0] ^ j
        q_out[:, pl.ds(pl.multiple_of(group * QW, LANES), QW)] = refs[j][...]
        o_out[:, pl.ds(pl.multiple_of(group * OW, LANES), OW)] = refs[N_GRP + j][...]


def call(kernel, outs, specs, scratch=(), vmem=32, flops=None):
    many = isinstance(outs, (list, tuple))
    return pl.pallas_call(
        kernel,
        out_shape=outs,
        in_specs=specs,
        out_specs=[VMEM] * len(outs) if many else VMEM,
        scratch_shapes=list(scratch),
        compiler_params=pltpu.CompilerParams(vmem_limit_bytes=vmem * MIB),
        cost_estimate=flops
        and pl.CostEstimate(flops=flops, bytes_accessed=4 * MIB, transcendentals=0),
    )


SWAP = [(0, 1), (1, 0)]


def to_groups(x):
    far = lax.ppermute(x, "xh", SWAP)
    return lax.ppermute(x, "core", SWAP), far, lax.ppermute(far, "core", SWAP)


def to_groups_at_once(x):
    return (
        lax.ppermute(x, "core", SWAP),
        lax.ppermute(x, "xh", SWAP),
        lax.ppermute(x, G_AXES, [(g, g ^ 3) for g in range(N_GRP)]),
    )


def exchange(x):
    rows = x.shape[0] // N_DEV
    x = x.reshape(N_DEV, rows, x.shape[1])
    x = lax.all_to_all(x, D_AXES, split_axis=0, concat_axis=0, tiled=True)
    return x.reshape(N_DEV * rows, x.shape[2])


def shards(hidden_in, w_qkv, w_o, key_cache, value_cache, lengths, finished, assignment):
    struct = jax.ShapeDtypeStruct
    group = lax.axis_index(G_AXES).astype(jnp.int32)
    dev = lax.axis_index(D_AXES).astype(jnp.int32)
    dev, group_one = dev.reshape(1), group.reshape(1)

    wq, wo = w_qkv.T, w_o.T
    far = lax.ppermute(wq, "xh", SWAP)
    both = lax.ppermute(jnp.stack([wq, far]), "core", SWAP)
    part = struct((N_DEV * ROWS, LANES), BF16)
    sent = call(
        pack_kernel,
        struct((N_DEV * PIECE, LANES), BF16),
        [SMEM] + [ANY] * 3,
        [
            pltpu.VMEM((ROWS, FEAT), BF16),
            pltpu.VMEM((WQ, D), BF16),
            pltpu.VMEM((WO, D), BF16),
            pltpu.VMEM((FULL, D), F32),
            pltpu.VMEM((MAIN, D), F32),
            pltpu.SemaphoreType.DMA((3,)),
        ],
        vmem=60,
    )(dev, hidden_in, wq, wo)
    recv = exchange(sent)
    sent = call(
        project_kernel,
        part,
        [SMEM, SMEM, VMEM, ANY] + [VMEM] * 2,
        [
            pltpu.VMEM((LANES, D), BF16),
            pltpu.VMEM((WQ, D), BF16),
            pltpu.SemaphoreType.DMA,
        ],
    )(dev, group_one, recv, wq, far, both)
    got = exchange(sent)

    o_block, lengths = call(
        turn_o_kernel,
        [struct((FEAT, OW), BF16), struct((ROWS, LANES), jnp.int32)],
        [SMEM, SMEM, VMEM, ANY],
        [pltpu.VMEM((OW, LANES), F32)],
    )(dev, lengths, recv, sent)
    o_blocks = (o_block,) + to_groups(o_block)

    q_block = call(
        turn_q_kernel,
        struct((FEAT, QW), BF16),
        [SMEM, VMEM, ANY],
        [pltpu.VMEM((QW, LANES), F32)],
    )(dev, recv, sent)
    q_blocks = (q_block,) + to_groups(q_block)
    cache = (ROWS * POS, KV_HEADS * LANES)
    tall = struct((KV_HEADS * GROUP, LANES), F32)
    scored = call(
        score_kernel,
        [tall] * 3 + [struct((KV_HEADS * ROWS, LANES), F32)],
        [SMEM] + [VMEM] * 3,
        flops=10**10,
    )(dev, lengths, got, key_cache.reshape(cache))
    sent = call(value_kernel, part, [VMEM] * 5, flops=10**10)(*scored, value_cache.reshape(cache))
    got = exchange(sent)
    sent = call(finish_kernel, part, [SMEM, SMEM] + [VMEM] * 5)(
        dev, group_one, got, *o_blocks
    )
    w_qkv_gen, w_o_gen, mark = call(
        order_kernel,
        [
            struct((FEAT, N_GRP * QW), BF16),
            struct((FEAT, N_GRP * OW), BF16),
            struct((ROWS, LANES), F32),
        ],
        [SMEM, ANY] + [VMEM] * 8,
    )(group_one, sent, *q_blocks, *o_blocks)
    got = exchange(sent)

    learners = jnp.arange(N_GRP, dtype=jnp.int32) ^ group
    matches = (assignment[None, :] == learners[:, None]) & (finished[None, :] == 1)
    ranks = jnp.cumsum(matches.astype(jnp.int32), axis=1)
    slots = jnp.arange(1, 3, dtype=jnp.int32)
    table = matches[:, None, :] & (ranks[:, None, :] == slots[None, :, None])
    table = table.reshape(ROWS, ROWS).astype(F32)
    few = struct((2, FEAT), F32)
    hidden_out, r0, r1, r2, r3 = call(
        total_kernel, [struct((ROWS, FEAT), F32)] + [few] * 4, [SMEM, VMEM, VMEM, ANY]
    )(dev, table, got, mark)
    r1 = lax.ppermute(r1, "core", SWAP)
    r2 = lax.ppermute(r2, "xh", SWAP)
    r3 = lax.ppermute(r3, G_AXES, [(g, g ^ 3) for g in range(N_GRP)])
    returned = jnp.concatenate(swapped_blocks((r0, r1, r2, r3), group), axis=0)
    return (hidden_out, returned, w_qkv_gen, w_o_gen)


def solution(mesh):
    fine = Mesh(mesh.devices.reshape(2, 2, 2, 4, 8), G_AXES + D_AXES)
    return jax.shard_map(
        shards,
        mesh=fine,
        in_specs=(
            P(G_AXES, D_AXES),
            P(None, G_AXES + D_AXES),
            P(None, G_AXES + D_AXES),
            P(G_AXES, D_AXES, None),
            P(G_AXES, D_AXES, None),
            P(G_AXES),
            P(G_AXES),
            P(G_AXES),
        ),
        out_specs=(P(G_AXES, D_AXES), P(G_AXES, D_AXES), P(D_AXES, None), P(D_AXES, None)),
        check_vma=False,
    )
```

```python
import functools
import math

import jax
import jax.numpy as jnp
from jax import lax
from jax.experimental import pallas as pl
from jax.experimental.pallas import tpu as pltpu
from jax.sharding import Mesh
from jax.sharding import PartitionSpec as P

N_DEV = 64
N_GRP = 4
ROWS = 8
HEADS = 40
KV_HEADS = 8
SHARE = HEADS // KV_HEADS
LANES = 128
D = 5120
FEAT = D // N_DEV
WQ = 28
WO = 20
FULL = WQ + WO
PIECE = 40
MAIN = PIECE - ROWS
QW = N_DEV * WQ
OW = N_DEV * WO
GROUP = ROWS * SHARE
WIDE = 48
POS = 128
NEG = -1e30

G_AXES = ("xh", "core")
D_AXES = ("xl", "y", "z")
F32 = jnp.float32
BF16 = jnp.bfloat16
VMEM = pl.BlockSpec(memory_space=pltpu.VMEM)
SMEM = pl.BlockSpec(memory_space=pltpu.SMEM)
ANY = pl.BlockSpec(memory_space=pl.ANY)
MIB = 1024 * 1024


def lane_iota(rows):
    return lax.broadcasted_iota(jnp.int32, (rows, LANES), 1)


def turned(lane, shift):
    return lane if shift % LANES == 0 else (lane - shift) & (LANES - 1)


def cut(tiles, start, width, lane):
    at, off = divmod(start, LANES)
    if off + width <= LANES:
        return tiles[at]
    return jnp.where(lane >= off, tiles[at], tiles[at + 1])


def lay(count, sources, width, lane):
    tiles = [None] * count
    for i, source in enumerate(sources):
        at, off = divmod(i * width, LANES)
        tiles[at] = source if tiles[at] is None else jnp.where(lane >= off, source, tiles[at])
        if off + width > LANES:
            tiles[at + 1] = source
    return tiles


def shift_of(dev, width):
    return (dev * width) & (LANES - 1)


def turned_back(x, shift):
    return pltpu.roll(x, (LANES - shift) & (LANES - 1), 1)


def halves(ref):
    parts = []
    for row in range(0, ref.shape[0], 16):
        both = ref[row : row + 16, :].astype(F32)
        parts += [both[0:8], both[8:16]]
    return parts


def pick(x, lanes):
    return jnp.take_along_axis(x, lanes, axis=1)


def swapped_blocks(blocks, group):
    odd = (group & 1) == 1
    high = (group & 2) == 2
    a, b, c, d = blocks
    a, b, c, d = (
        jnp.where(odd, b, a),
        jnp.where(odd, a, b),
        jnp.where(odd, d, c),
        jnp.where(odd, c, d),
    )
    return (
        jnp.where(high, c, a),
        jnp.where(high, d, b),
        jnp.where(high, a, c),
        jnp.where(high, b, d),
    )


def pack_kernel(
    dev_ref, hidden_hbm, wq_hbm, wo_hbm, out_ref, hidden_ref, wq_ref, wo_ref, rows_ref, spare_ref, sems
):
    copies = [pltpu.make_async_copy(hidden_hbm, hidden_ref, sems.at[0])]
    for h in range(2):
        half = pl.ds(h * D // 2, D // 2)
        for i, (source, target) in enumerate(((wq_hbm, wq_ref), (wo_hbm, wo_ref))):
            copies.append(
                pltpu.make_async_copy(
                    source.at[:, half], target.at[:, half], sems.at[1 + 2 * h + i]
                )
            )
    for copy in copies:
        copy.start()
    lane = lane_iota(MAIN)
    copies[0].wait()
    hidden = jnp.concatenate(
        [hidden_ref[...].astype(F32), jnp.zeros((ROWS, LANES - FEAT), F32)], axis=1
    )
    hidden = pltpu.roll(hidden, shift_of(dev_ref[0], FEAT), 1)
    half = lane[0:16]
    from_spare = jnp.concatenate([turned(half, FEAT), turned(half, 2 * FEAT - LANES)], axis=0)
    pair = []
    for dest in range(N_DEV):
        if dest % (N_DEV // 2) == 0:
            h = dest // (N_DEV // 2)
            columns = slice(h * D // 2, (h + 1) * D // 2)
            copies[1 + 2 * h].wait()
            rows_ref[0:WQ, columns] = wq_ref[:, columns].astype(F32)
            copies[2 + 2 * h].wait()
            rows_ref[WQ:FULL, columns] = wo_ref[:, columns].astype(F32)
            for t in range(h * D // 2 // LANES, (h + 1) * D // 2 // LANES):
                columns = slice(t * LANES, (t + 1) * LANES)
                rest = rows_ref[MAIN:FULL, columns]
                spare_ref[0:16, columns] = pltpu.roll(rest, FEAT, 1)
                spare_ref[16:32, columns] = pltpu.roll(rest, 2 * FEAT - LANES, 1)
        at, off = divmod(dest * FEAT, LANES)
        main = {t: rows_ref[0:MAIN, t * LANES : (t + 1) * LANES] for t in (at, at + 1) if t < D // LANES}
        spare = {t: spare_ref[:, t * LANES : (t + 1) * LANES] for t in (at, at + 1) if t < D // LANES}
        piece = jnp.where(
            turned(lane, off) < FEAT,
            cut(main, dest * FEAT, FEAT, lane),
            cut(spare, dest * FEAT, FEAT, from_spare),
        )
        pair += [hidden, piece]
        if dest % 2:
            out_ref[(dest - 1) * PIECE : (dest + 1) * PIECE, :] = jnp.concatenate(
                pair, axis=0
            ).astype(BF16)
            pair = []


def merge_kernel(own_ref, far_ref, both_ref, out_ref):
    for j, ref in enumerate((own_ref, both_ref.at[0], far_ref, both_ref.at[1])):
        out_ref[32 * j + 16 : 32 * j + 32, :] = jnp.zeros((16, D), BF16)
        out_ref[32 * j : 32 * j + WQ, :] = ref[...]


def project_kernel(dev_ref, group_ref, recv_ref, w_ref, out_ref):
    lane = lane_iota(ROWS)
    dev, group = dev_ref[0], group_ref[0]
    sources = []
    for source in range(N_DEV):
        row = source * PIECE - source * PIECE % 16
        both = recv_ref[row : row + 16, :].astype(F32)
        sources.append(both[8:16] if source % 2 else both[0:8])
    tiles = lay(D // LANES, sources, FEAT, lane)
    hidden = jnp.concatenate([t.astype(BF16) for t in tiles], axis=1)
    y = lax.dot_general(hidden, w_ref[...], (((1,), (1,)), ((), ())), preferred_element_type=F32)
    up, down = pltpu.roll(y, 32, 1), pltpu.roll(y, LANES - 32, 1)
    y = jnp.where((group & 1) == 1, jnp.where((lane & 32) == 0, down, up), y)
    y = jnp.where((group & 2) == 2, pltpu.roll(y, 64, 1), y)
    y = pltpu.roll(y, shift_of(dev, WQ), 1)
    two = jnp.concatenate([y, y], axis=0).astype(BF16)
    for pair in range(N_DEV // 2):
        out_ref[16 * pair : 16 * pair + 16, :] = two


def turn(dev, x):
    row = lax.broadcasted_iota(jnp.int32, (FEAT, LANES), 0)
    eye = (((row + shift_of(dev, FEAT)) & (LANES - 1)) == lane_iota(FEAT)).astype(BF16)
    return lax.dot_general(
        eye, x.astype(BF16), (((1,), (1,)), ((), ())), preferred_element_type=F32
    ).astype(BF16)


def turn_o_kernel(dev_ref, lengths_ref, recv_ref, after_ref, out_ref, wide_ref, rows_ref):
    for r in range(ROWS):
        wide_ref[r : r + 1, :] = jnp.full((1, LANES), lengths_ref[r], jnp.int32)
    shift = shift_of(dev_ref[0], FEAT)
    first = ((lane_iota(16) - shift) & (LANES - 1)) < LANES - FEAT
    for source in range(N_DEV):
        if source % 2 == 0:
            both = recv_ref[source * PIECE : (source + 2) * PIECE, :].astype(F32)
        piece = both[source % 2 * PIECE + ROWS : (source % 2 + 1) * PIECE]
        rest = jnp.where(
            first,
            pltpu.roll(piece[0:16], LANES - FEAT, 1),
            pltpu.roll(piece[16:32], 2 * LANES - 2 * FEAT, 1),
        )
        rows_ref[source * WO : source * WO + MAIN - WQ, :] = piece[WQ:MAIN]
        rows_ref[source * WO + MAIN - WQ : (source + 1) * WO, :] = rest
    out_ref[...] = turn(dev_ref[0], rows_ref[...])


def turn_q_kernel(dev_ref, recv_ref, after_ref, out_ref, rows_ref):
    for source in range(N_DEV):
        if source % 2 == 0:
            both = recv_ref[source * PIECE : (source + 2) * PIECE, :].astype(F32)
        piece = both[source % 2 * PIECE + ROWS : (source % 2 + 1) * PIECE]
        rows_ref[source * WQ : (source + 1) * WQ, :] = piece[0:WQ]
    out_ref[...] = turn(dev_ref[0], rows_ref[...])


def score_kernel(
    dev_ref, lengths_ref, recv_ref, keys_ref, spread_ref, own_ref, tag_ref, fresh_ref
):
    lane = lane_iota(ROWS)
    sub = lax.broadcasted_iota(jnp.int32, (ROWS, LANES), 0)
    dev = dev_ref[0]
    scale = 1.0 / math.sqrt(LANES)
    sources = halves(recv_ref)
    tiles = []
    for g in range(N_GRP):
        frame = lay(QW // LANES, sources, WQ, turned(lane, 32 * g))
        tiles += [pltpu.roll(t, LANES - 32 * g, 1) for t in frame] if g else frame
    own_rows = [sub == r for r in range(ROWS)]
    valid = dev * POS + lane < lengths_ref[...]
    valid = jnp.concatenate([valid] * SHARE, axis=0)
    first = dev == 0
    at = lane_iota(GROUP) & 7
    for k in range(KV_HEADS):
        new_key = tiles[HEADS + k]
        q = jnp.concatenate(tiles[k * SHARE : (k + 1) * SHARE], axis=0)
        keys = keys_ref[:, k * LANES : (k + 1) * LANES]
        wide = lax.dot_general(
            q.astype(BF16), keys, (((1,), (1,)), ((), ())), preferred_element_type=F32
        )
        s = []
        for i in range(SHARE):
            line = wide[i * ROWS : (i + 1) * ROWS, 0:LANES]
            for r in range(1, ROWS):
                line = jnp.where(
                    own_rows[r],
                    wide[i * ROWS : (i + 1) * ROWS, r * LANES : (r + 1) * LANES],
                    line,
                )
            s.append(line)
        s = jnp.concatenate(s, axis=0) * scale
        s = jnp.where(valid, s, NEG)
        own = jnp.sum(q * jnp.concatenate([new_key] * SHARE, axis=0), axis=1, keepdims=True) * scale
        own = jnp.where(first, own, NEG)
        top = jnp.maximum(jnp.max(s, axis=1, keepdims=True), own)
        w = jnp.where(valid, jnp.exp(s - top), 0.0)
        own_w = jnp.where(first, jnp.exp(own - top), 0.0)
        total = jnp.sum(w, axis=1, keepdims=True) + own_w
        rows = slice(k * GROUP, (k + 1) * GROUP)
        for r in range(ROWS):
            spread_ref[k * WIDE : k * WIDE + GROUP, r * LANES : (r + 1) * LANES] = jnp.concatenate(
                [
                    jnp.where(own_rows[r], w[i * ROWS : (i + 1) * ROWS], 0.0)
                    for i in range(SHARE)
                ],
                axis=0,
            ).astype(BF16)
        own_ref[rows, :] = jnp.broadcast_to(own_w, (GROUP, LANES))
        t = jnp.broadcast_to(top, (GROUP, LANES))
        t0 = t.astype(BF16).astype(F32)
        t1 = (t - t0).astype(BF16).astype(F32)
        d = jnp.broadcast_to(total, (GROUP, LANES))
        d0 = d.astype(BF16).astype(F32)
        tag = jnp.where(at == 0, t0, jnp.where(at == 1, t1, (t - t0) - t1))
        tag_ref[rows, :] = jnp.where(at < 3, tag, jnp.where(at == 3, d0, d - d0))
        fresh_ref[k * ROWS : (k + 1) * ROWS, :] = tiles[HEADS + KV_HEADS + k]


def value_kernel(spread_ref, own_ref, tag_ref, fresh_ref, values_ref, out_ref):
    lane = lane_iota(ROWS)
    outs, tags = [], []
    for k in range(KV_HEADS):
        heads = [slice(k * GROUP + i * ROWS, k * GROUP + (i + 1) * ROWS) for i in range(SHARE)]
        values = values_ref[:, k * LANES : (k + 1) * LANES]
        out = jnp.dot(
            spread_ref[k * WIDE : (k + 1) * WIDE, :], values, preferred_element_type=F32
        )
        fresh = fresh_ref[k * ROWS : (k + 1) * ROWS, :]
        for i, h in enumerate(heads):
            outs.append(out[i * ROWS : (i + 1) * ROWS] + own_ref[h, :] * fresh)
            tags.append(tag_ref[h, :])
    pair = []
    for dest in range(N_DEV):
        h0, h1 = dest * FEAT // LANES, (dest * FEAT + FEAT - 1) // LANES
        tile = cut(outs, dest * FEAT, FEAT, lane)
        place = turned(lane, dest * FEAT)
        tile = jnp.where(place < FEAT, tile, jnp.where(place < FEAT + 8, tags[h0], tags[h1]))
        pair.append(tile)
        if dest % 2:
            out_ref[(dest - 1) * ROWS : (dest + 1) * ROWS, :] = jnp.concatenate(
                pair, axis=0
            ).astype(BF16)
            pair = []


def finish_kernel(dev_ref, group_ref, recv_ref, b0_ref, b1_ref, b2_ref, b3_ref, out_ref):
    lane = lane_iota(ROWS)
    dev, group = dev_ref[0], group_ref[0]
    start = dev * FEAT
    split = ((start + FEAT - 1) // LANES) * LANES - start
    split = jnp.where(split <= 0, FEAT, split)
    shift = shift_of(dev, FEAT)
    spot = (lane - shift) & (LANES - 1)
    left = (spot < split) | ((spot >= FEAT) & (spot < FEAT + 8))
    tag = jnp.where(left, FEAT, FEAT + 8) + shift
    at = [(tag + i) & (LANES - 1) for i in range(5)]
    parts = halves(recv_ref)
    tops = [(pick(x, at[0]) + pick(x, at[1])) + pick(x, at[2]) for x in parts]
    top = tops
    while len(top) > 1:
        top = [jnp.maximum(a, b) for a, b in zip(top[0::2], top[1::2])]
    total = [jnp.zeros((ROWS, LANES), F32) for _ in range(4)]
    for s, part in enumerate(parts):
        total[s % 4] = total[s % 4] + jnp.exp(tops[s] - top[0]) * part
    total = (total[0] + total[1]) + (total[2] + total[3])
    den = pick(total, at[3]) + pick(total, at[4])
    attn = turned_back(total / den, shift)[:, 0:FEAT].astype(BF16)
    blocks = [
        jnp.dot(attn, ref[...], preferred_element_type=F32)
        for ref in (b0_ref, b1_ref, b2_ref, b3_ref)
    ]
    blocks = swapped_blocks(blocks, group)
    tiles = [
        block[:, t * LANES : (t + 1) * LANES] for block in blocks for t in range(OW // LANES)
    ]
    for dest in range(0, N_DEV, 2):
        pair = [cut(tiles, d * FEAT, FEAT, lane) for d in (dest, dest + 1)]
        out_ref[dest * ROWS : (dest + 2) * ROWS, :] = jnp.concatenate(pair, axis=0).astype(BF16)


def total_kernel(dev_ref, table_ref, recv_ref, after_ref, hidden_ref, r0_ref, r1_ref, r2_ref, r3_ref):
    sums = halves(recv_ref)
    while len(sums) > 1:
        sums = [a + b for a, b in zip(sums[0::2], sums[1::2])]
    hidden = turned_back(sums[0], shift_of(dev_ref[0], FEAT))
    hidden_ref[...] = hidden[:, 0:FEAT]
    table = table_ref[...]
    packed = table[:, 0:1] * hidden[0:1, :]
    for r in range(1, ROWS):
        packed = packed + table[:, r : r + 1] * hidden[r : r + 1, :]
    for j, ref in enumerate((r0_ref, r1_ref, r2_ref, r3_ref)):
        ref[...] = packed[2 * j : 2 * j + 2, 0:FEAT]


def order_kernel(group_ref, after_ref, *refs):
    q_out, o_out, mark_ref = refs[8:]
    mark_ref[...] = jnp.zeros_like(mark_ref)
    for j in range(N_GRP):
        group = group_ref[0] ^ j
        q_out[:, pl.ds(pl.multiple_of(group * QW, LANES), QW)] = refs[j][...]
        o_out[:, pl.ds(pl.multiple_of(group * OW, LANES), OW)] = refs[N_GRP + j][...]


def call(kernel, outs, specs, scratch=(), vmem=32, flops=None):
    many = isinstance(outs, (list, tuple))
    return pl.pallas_call(
        kernel,
        out_shape=outs,
        in_specs=specs,
        out_specs=[VMEM] * len(outs) if many else VMEM,
        scratch_shapes=list(scratch),
        compiler_params=pltpu.CompilerParams(vmem_limit_bytes=vmem * MIB),
        cost_estimate=flops
        and pl.CostEstimate(flops=flops, bytes_accessed=4 * MIB, transcendentals=0),
    )


SWAP = [(0, 1), (1, 0)]


def to_groups(x):
    far = lax.ppermute(x, "xh", SWAP)
    return lax.ppermute(x, "core", SWAP), far, lax.ppermute(far, "core", SWAP)


def to_groups_at_once(x):
    return (
        lax.ppermute(x, "core", SWAP),
        lax.ppermute(x, "xh", SWAP),
        lax.ppermute(x, G_AXES, [(g, g ^ 3) for g in range(N_GRP)]),
    )


def exchange(x):
    rows = x.shape[0] // N_DEV
    x = x.reshape(N_DEV, rows, x.shape[1])
    x = lax.all_to_all(x, D_AXES, split_axis=0, concat_axis=0, tiled=True)
    return x.reshape(N_DEV * rows, x.shape[2])


def shards(hidden_in, w_qkv, w_o, key_cache, value_cache, lengths, finished, assignment):
    struct = jax.ShapeDtypeStruct
    group = lax.axis_index(G_AXES).astype(jnp.int32)
    dev = lax.axis_index(D_AXES).astype(jnp.int32)
    dev, group_one = dev.reshape(1), group.reshape(1)

    wq, wo = w_qkv.T, w_o.T
    far = lax.ppermute(wq, "xh", SWAP)
    both = lax.ppermute(jnp.stack([wq, far]), "core", SWAP)
    part = struct((N_DEV * ROWS, LANES), BF16)
    sent = call(
        pack_kernel,
        struct((N_DEV * PIECE, LANES), BF16),
        [SMEM] + [ANY] * 3,
        [
            pltpu.VMEM((ROWS, FEAT), BF16),
            pltpu.VMEM((WQ, D), BF16),
            pltpu.VMEM((WO, D), BF16),
            pltpu.VMEM((FULL, D), F32),
            pltpu.VMEM((MAIN, D), F32),
            pltpu.SemaphoreType.DMA((5,)),
        ],
        vmem=60,
    )(dev, hidden_in, wq, wo)
    recv = exchange(sent)
    merged = call(merge_kernel, struct((LANES, D), BF16), [VMEM] * 3)(wq, far, both)
    sent = call(project_kernel, part, [SMEM, SMEM, VMEM, VMEM])(dev, group_one, recv, merged)
    got = exchange(sent)

    o_block, lengths = call(
        turn_o_kernel,
        [struct((FEAT, OW), BF16), struct((ROWS, LANES), jnp.int32)],
        [SMEM, SMEM, VMEM, ANY],
        [pltpu.VMEM((OW, LANES), F32)],
    )(dev, lengths, recv, sent)
    o_blocks = (o_block,) + to_groups(o_block)

    q_block = call(
        turn_q_kernel,
        struct((FEAT, QW), BF16),
        [SMEM, VMEM, ANY],
        [pltpu.VMEM((QW, LANES), F32)],
    )(dev, recv, sent)
    q_blocks = (q_block,) + to_groups(q_block)
    cache = (ROWS * POS, KV_HEADS * LANES)
    tall = struct((KV_HEADS * GROUP, LANES), F32)
    scored = call(
        score_kernel,
        [struct((KV_HEADS * WIDE, ROWS * POS), BF16), tall, tall]
        + [struct((KV_HEADS * ROWS, LANES), F32)],
        [SMEM] + [VMEM] * 3,
        flops=10**10,
    )(dev, lengths, got, key_cache.reshape(cache))
    sent = call(value_kernel, part, [VMEM] * 5, flops=10**10)(*scored, value_cache.reshape(cache))
    got = exchange(sent)
    sent = call(finish_kernel, part, [SMEM, SMEM] + [VMEM] * 5)(
        dev, group_one, got, *o_blocks
    )
    w_qkv_gen, w_o_gen, mark = call(
        order_kernel,
        [
            struct((FEAT, N_GRP * QW), BF16),
            struct((FEAT, N_GRP * OW), BF16),
            struct((ROWS, LANES), F32),
        ],
        [SMEM, ANY] + [VMEM] * 8,
    )(group_one, sent, *q_blocks, *o_blocks)
    got = exchange(sent)

    learners = jnp.arange(N_GRP, dtype=jnp.int32) ^ group
    matches = (assignment[None, :] == learners[:, None]) & (finished[None, :] == 1)
    ranks = jnp.cumsum(matches.astype(jnp.int32), axis=1)
    slots = jnp.arange(1, 3, dtype=jnp.int32)
    table = matches[:, None, :] & (ranks[:, None, :] == slots[None, :, None])
    table = table.reshape(ROWS, ROWS).astype(F32)
    few = struct((2, FEAT), F32)
    hidden_out, r0, r1, r2, r3 = call(
        total_kernel, [struct((ROWS, FEAT), F32)] + [few] * 4, [SMEM, VMEM, VMEM, ANY]
    )(dev, table, got, mark)
    r1 = lax.ppermute(r1, "core", SWAP)
    r2 = lax.ppermute(r2, "xh", SWAP)
    r3 = lax.ppermute(r3, G_AXES, [(g, g ^ 3) for g in range(N_GRP)])
    returned = jnp.concatenate(swapped_blocks((r0, r1, r2, r3), group), axis=0)
    return (hidden_out, returned, w_qkv_gen, w_o_gen)


def solution(mesh):
    fine = Mesh(mesh.devices.reshape(2, 2, 2, 4, 8), G_AXES + D_AXES)
    return jax.shard_map(
        shards,
        mesh=fine,
        in_specs=(
            P(G_AXES, D_AXES),
            P(None, G_AXES + D_AXES),
            P(None, G_AXES + D_AXES),
            P(G_AXES, D_AXES, None),
            P(G_AXES, D_AXES, None),
            P(G_AXES),
            P(G_AXES),
            P(G_AXES),
        ),
        out_specs=(P(G_AXES, D_AXES), P(G_AXES, D_AXES), P(D_AXES, None), P(D_AXES, None)),
        check_vma=False,
    )
```

```python
import functools
import math

import jax
import jax.numpy as jnp
from jax import lax
from jax.experimental import pallas as pl
from jax.experimental.pallas import tpu as pltpu
from jax.sharding import Mesh
from jax.sharding import PartitionSpec as P

N_DEV = 64
N_GRP = 4
ROWS = 8
HEADS = 40
KV_HEADS = 8
SHARE = HEADS // KV_HEADS
LANES = 128
D = 5120
FEAT = D // N_DEV
WQ = 28
WO = 20
FULL = WQ + WO
PIECE = 40
MAIN = PIECE - ROWS
QW = N_DEV * WQ
OW = N_DEV * WO
GROUP = ROWS * SHARE
WIDE = 48
POS = 128
NEG = -1e30

G_AXES = ("xh", "core")
D_AXES = ("xl", "y", "z")
F32 = jnp.float32
BF16 = jnp.bfloat16
VMEM = pl.BlockSpec(memory_space=pltpu.VMEM)
SMEM = pl.BlockSpec(memory_space=pltpu.SMEM)
ANY = pl.BlockSpec(memory_space=pl.ANY)
MIB = 1024 * 1024


def lane_iota(rows):
    return lax.broadcasted_iota(jnp.int32, (rows, LANES), 1)


def turned(lane, shift):
    return lane if shift % LANES == 0 else (lane - shift) & (LANES - 1)


def cut(tiles, start, width, lane):
    at, off = divmod(start, LANES)
    if off + width <= LANES:
        return tiles[at]
    return jnp.where(lane >= off, tiles[at], tiles[at + 1])


def lay(count, sources, width, lane):
    tiles = [None] * count
    for i, source in enumerate(sources):
        at, off = divmod(i * width, LANES)
        tiles[at] = source if tiles[at] is None else jnp.where(lane >= off, source, tiles[at])
        if off + width > LANES:
            tiles[at + 1] = source
    return tiles


def shift_of(dev, width):
    return (dev * width) & (LANES - 1)


def turned_back(x, shift):
    return pltpu.roll(x, (LANES - shift) & (LANES - 1), 1)


def halves(ref):
    parts = []
    for row in range(0, ref.shape[0], 16):
        both = ref[row : row + 16, :].astype(F32)
        parts += [both[0:8], both[8:16]]
    return parts


def pick(x, lanes):
    return jnp.take_along_axis(x, lanes, axis=1)


def swapped_blocks(blocks, group):
    odd = (group & 1) == 1
    high = (group & 2) == 2
    a, b, c, d = blocks
    a, b, c, d = (
        jnp.where(odd, b, a),
        jnp.where(odd, a, b),
        jnp.where(odd, d, c),
        jnp.where(odd, c, d),
    )
    return (
        jnp.where(high, c, a),
        jnp.where(high, d, b),
        jnp.where(high, a, c),
        jnp.where(high, b, d),
    )


def pack_kernel(
    dev_ref, hidden_hbm, wq_hbm, wo_hbm, out_ref, hidden_ref, wq_ref, wo_ref, rows_ref, spare_ref, sems
):
    copies = [pltpu.make_async_copy(hidden_hbm, hidden_ref, sems.at[0])]
    for h in range(2):
        half = pl.ds(h * D // 2, D // 2)
        for i, (source, target) in enumerate(((wq_hbm, wq_ref), (wo_hbm, wo_ref))):
            copies.append(
                pltpu.make_async_copy(
                    source.at[:, half], target.at[:, half], sems.at[1 + 2 * h + i]
                )
            )
    for copy in copies:
        copy.start()
    lane = lane_iota(MAIN)
    copies[0].wait()
    hidden = jnp.concatenate(
        [hidden_ref[...].astype(F32), jnp.zeros((ROWS, LANES - FEAT), F32)], axis=1
    )
    hidden = pltpu.roll(hidden, shift_of(dev_ref[0], FEAT), 1)
    half = lane[0:16]
    from_spare = jnp.concatenate([turned(half, FEAT), turned(half, 2 * FEAT - LANES)], axis=0)
    pair = []
    for dest in range(N_DEV):
        if dest % (N_DEV // 2) == 0:
            h = dest // (N_DEV // 2)
            columns = slice(h * D // 2, (h + 1) * D // 2)
            copies[1 + 2 * h].wait()
            rows_ref[0:WQ, columns] = wq_ref[:, columns].astype(F32)
            copies[2 + 2 * h].wait()
            rows_ref[WQ:FULL, columns] = wo_ref[:, columns].astype(F32)
            for t in range(h * D // 2 // LANES, (h + 1) * D // 2 // LANES):
                columns = slice(t * LANES, (t + 1) * LANES)
                rest = rows_ref[MAIN:FULL, columns]
                spare_ref[0:16, columns] = pltpu.roll(rest, FEAT, 1)
                spare_ref[16:32, columns] = pltpu.roll(rest, 2 * FEAT - LANES, 1)
        at, off = divmod(dest * FEAT, LANES)
        main = {t: rows_ref[0:MAIN, t * LANES : (t + 1) * LANES] for t in (at, at + 1) if t < D // LANES}
        spare = {t: spare_ref[:, t * LANES : (t + 1) * LANES] for t in (at, at + 1) if t < D // LANES}
        piece = jnp.where(
            turned(lane, off) < FEAT,
            cut(main, dest * FEAT, FEAT, lane),
            cut(spare, dest * FEAT, FEAT, from_spare),
        )
        pair += [hidden, piece]
        if dest % 2:
            out_ref[(dest - 1) * PIECE : (dest + 1) * PIECE, :] = jnp.concatenate(
                pair, axis=0
            ).astype(BF16)
            pair = []


def merge_kernel(own_ref, far_ref, both_ref, out_ref):
    for j, ref in enumerate((own_ref, both_ref.at[0], far_ref, both_ref.at[1])):
        out_ref[32 * j + 16 : 32 * j + 32, :] = jnp.zeros((16, D), BF16)
        out_ref[32 * j : 32 * j + WQ, :] = ref[...]


def project_kernel(dev_ref, group_ref, recv_ref, w_ref, out_ref):
    lane = lane_iota(ROWS)
    dev, group = dev_ref[0], group_ref[0]
    sources = []
    for source in range(N_DEV):
        row = source * PIECE - source * PIECE % 16
        both = recv_ref[row : row + 16, :].astype(F32)
        sources.append(both[8:16] if source % 2 else both[0:8])
    tiles = lay(D // LANES, sources, FEAT, lane)
    hidden = jnp.concatenate([t.astype(BF16) for t in tiles], axis=1)
    y = lax.dot_general(hidden, w_ref[...], (((1,), (1,)), ((), ())), preferred_element_type=F32)
    up, down = pltpu.roll(y, 32, 1), pltpu.roll(y, LANES - 32, 1)
    y = jnp.where((group & 1) == 1, jnp.where((lane & 32) == 0, down, up), y)
    y = jnp.where((group & 2) == 2, pltpu.roll(y, 64, 1), y)
    y = pltpu.roll(y, shift_of(dev, WQ), 1)
    two = jnp.concatenate([y, y], axis=0).astype(BF16)
    for pair in range(N_DEV // 2):
        out_ref[16 * pair : 16 * pair + 16, :] = two


def turn(dev, x):
    row = lax.broadcasted_iota(jnp.int32, (FEAT, LANES), 0)
    eye = (((row + shift_of(dev, FEAT)) & (LANES - 1)) == lane_iota(FEAT)).astype(BF16)
    return lax.dot_general(
        eye, x.astype(BF16), (((1,), (1,)), ((), ())), preferred_element_type=F32
    ).astype(BF16)


def turn_o_kernel(dev_ref, lengths_ref, recv_ref, after_ref, out_ref, wide_ref, rows_ref):
    for r in range(ROWS):
        wide_ref[r : r + 1, :] = jnp.full((1, LANES), lengths_ref[r], jnp.int32)
    shift = shift_of(dev_ref[0], FEAT)
    first = ((lane_iota(16) - shift) & (LANES - 1)) < LANES - FEAT
    for source in range(N_DEV):
        if source % 2 == 0:
            both = recv_ref[source * PIECE : (source + 2) * PIECE, :].astype(F32)
        piece = both[source % 2 * PIECE + ROWS : (source % 2 + 1) * PIECE]
        rest = jnp.where(
            first,
            pltpu.roll(piece[0:16], LANES - FEAT, 1),
            pltpu.roll(piece[16:32], 2 * LANES - 2 * FEAT, 1),
        )
        rows_ref[source * WO : source * WO + MAIN - WQ, :] = piece[WQ:MAIN]
        rows_ref[source * WO + MAIN - WQ : (source + 1) * WO, :] = rest
    out_ref[...] = turn(dev_ref[0], rows_ref[...])


def turn_q_kernel(dev_ref, recv_ref, after_ref, out_ref, rows_ref):
    for source in range(N_DEV):
        if source % 2 == 0:
            both = recv_ref[source * PIECE : (source + 2) * PIECE, :].astype(F32)
        piece = both[source % 2 * PIECE + ROWS : (source % 2 + 1) * PIECE]
        rows_ref[source * WQ : (source + 1) * WQ, :] = piece[0:WQ]
    out_ref[...] = turn(dev_ref[0], rows_ref[...])


def query_kernel(recv_ref, out_ref):
    lane = lane_iota(ROWS)
    sources = halves(recv_ref)
    for g in range(N_GRP):
        frame = lay(QW // LANES, sources, WQ, turned(lane, 32 * g))
        for t, tile in enumerate(frame):
            row = (g * len(frame) + t) * ROWS
            out_ref[row : row + ROWS, :] = pltpu.roll(tile, LANES - 32 * g, 1) if g else tile


def score_kernel(
    dev_ref, lengths_ref, tiles_ref, keys_ref, spread_ref, own_ref, tag_ref, fresh_ref
):
    lane = lane_iota(ROWS)
    sub = lax.broadcasted_iota(jnp.int32, (ROWS, LANES), 0)
    dev = dev_ref[0]
    scale = 1.0 / math.sqrt(LANES)
    tiles = [tiles_ref[h * ROWS : (h + 1) * ROWS, :] for h in range(HEADS + 2 * KV_HEADS)]
    own_rows = [sub == r for r in range(ROWS)]
    valid = dev * POS + lane < lengths_ref[...]
    valid = jnp.concatenate([valid] * SHARE, axis=0)
    first = dev == 0
    at = lane_iota(GROUP) & 7
    for k in range(KV_HEADS):
        new_key = tiles[HEADS + k]
        q = jnp.concatenate(tiles[k * SHARE : (k + 1) * SHARE], axis=0)
        keys = keys_ref[:, k * LANES : (k + 1) * LANES]
        wide = lax.dot_general(
            q.astype(BF16), keys, (((1,), (1,)), ((), ())), preferred_element_type=F32
        )
        s = []
        for i in range(SHARE):
            line = wide[i * ROWS : (i + 1) * ROWS, 0:LANES]
            for r in range(1, ROWS):
                line = jnp.where(
                    own_rows[r],
                    wide[i * ROWS : (i + 1) * ROWS, r * LANES : (r + 1) * LANES],
                    line,
                )
            s.append(line)
        s = jnp.concatenate(s, axis=0) * scale
        s = jnp.where(valid, s, NEG)
        own = jnp.sum(q * jnp.concatenate([new_key] * SHARE, axis=0), axis=1, keepdims=True) * scale
        own = jnp.where(first, own, NEG)
        top = jnp.maximum(jnp.max(s, axis=1, keepdims=True), own)
        w = jnp.where(valid, jnp.exp(s - top), 0.0)
        own_w = jnp.where(first, jnp.exp(own - top), 0.0)
        total = jnp.sum(w, axis=1, keepdims=True) + own_w
        rows = slice(k * GROUP, (k + 1) * GROUP)
        for r in range(ROWS):
            spread_ref[k * WIDE : k * WIDE + GROUP, r * LANES : (r + 1) * LANES] = jnp.concatenate(
                [
                    jnp.where(own_rows[r], w[i * ROWS : (i + 1) * ROWS], 0.0)
                    for i in range(SHARE)
                ],
                axis=0,
            ).astype(BF16)
        own_ref[rows, :] = jnp.broadcast_to(own_w, (GROUP, LANES))
        t = jnp.broadcast_to(top, (GROUP, LANES))
        t0 = t.astype(BF16).astype(F32)
        t1 = (t - t0).astype(BF16).astype(F32)
        d = jnp.broadcast_to(total, (GROUP, LANES))
        d0 = d.astype(BF16).astype(F32)
        tag = jnp.where(at == 0, t0, jnp.where(at == 1, t1, (t - t0) - t1))
        tag_ref[rows, :] = jnp.where(at < 3, tag, jnp.where(at == 3, d0, d - d0))
        fresh_ref[k * ROWS : (k + 1) * ROWS, :] = tiles[HEADS + KV_HEADS + k]


def value_kernel(spread_ref, own_ref, tag_ref, fresh_ref, values_ref, out_ref):
    lane = lane_iota(ROWS)
    outs, tags = [], []
    for k in range(KV_HEADS):
        heads = [slice(k * GROUP + i * ROWS, k * GROUP + (i + 1) * ROWS) for i in range(SHARE)]
        values = values_ref[:, k * LANES : (k + 1) * LANES]
        out = jnp.dot(
            spread_ref[k * WIDE : (k + 1) * WIDE, :], values, preferred_element_type=F32
        )
        fresh = fresh_ref[k * ROWS : (k + 1) * ROWS, :]
        for i, h in enumerate(heads):
            outs.append(out[i * ROWS : (i + 1) * ROWS] + own_ref[h, :] * fresh)
            tags.append(tag_ref[h, :])
    pair = []
    for dest in range(N_DEV):
        h0, h1 = dest * FEAT // LANES, (dest * FEAT + FEAT - 1) // LANES
        tile = cut(outs, dest * FEAT, FEAT, lane)
        place = turned(lane, dest * FEAT)
        tile = jnp.where(place < FEAT, tile, jnp.where(place < FEAT + 8, tags[h0], tags[h1]))
        pair.append(tile)
        if dest % 2:
            out_ref[(dest - 1) * ROWS : (dest + 1) * ROWS, :] = jnp.concatenate(
                pair, axis=0
            ).astype(BF16)
            pair = []


def finish_kernel(dev_ref, group_ref, recv_ref, b0_ref, b1_ref, b2_ref, b3_ref, out_ref):
    lane = lane_iota(ROWS)
    dev, group = dev_ref[0], group_ref[0]
    start = dev * FEAT
    split = ((start + FEAT - 1) // LANES) * LANES - start
    split = jnp.where(split <= 0, FEAT, split)
    shift = shift_of(dev, FEAT)
    spot = (lane - shift) & (LANES - 1)
    left = (spot < split) | ((spot >= FEAT) & (spot < FEAT + 8))
    tag = jnp.where(left, FEAT, FEAT + 8) + shift
    at = [(tag + i) & (LANES - 1) for i in range(5)]
    parts = halves(recv_ref)
    tops = [(pick(x, at[0]) + pick(x, at[1])) + pick(x, at[2]) for x in parts]
    top = tops
    while len(top) > 1:
        top = [jnp.maximum(a, b) for a, b in zip(top[0::2], top[1::2])]
    total = [jnp.zeros((ROWS, LANES), F32) for _ in range(4)]
    for s, part in enumerate(parts):
        total[s % 4] = total[s % 4] + jnp.exp(tops[s] - top[0]) * part
    total = (total[0] + total[1]) + (total[2] + total[3])
    den = pick(total, at[3]) + pick(total, at[4])
    attn = turned_back(total / den, shift)[:, 0:FEAT].astype(BF16)
    blocks = [
        jnp.dot(attn, ref[...], preferred_element_type=F32)
        for ref in (b0_ref, b1_ref, b2_ref, b3_ref)
    ]
    blocks = swapped_blocks(blocks, group)
    tiles = [
        block[:, t * LANES : (t + 1) * LANES] for block in blocks for t in range(OW // LANES)
    ]
    for dest in range(0, N_DEV, 2):
        pair = [cut(tiles, d * FEAT, FEAT, lane) for d in (dest, dest + 1)]
        out_ref[dest * ROWS : (dest + 2) * ROWS, :] = jnp.concatenate(pair, axis=0).astype(BF16)


def total_kernel(dev_ref, table_ref, recv_ref, after_ref, hidden_ref, r0_ref, r1_ref, r2_ref, r3_ref):
    sums = halves(recv_ref)
    while len(sums) > 1:
        sums = [a + b for a, b in zip(sums[0::2], sums[1::2])]
    hidden = turned_back(sums[0], shift_of(dev_ref[0], FEAT))
    hidden_ref[...] = hidden[:, 0:FEAT]
    table = table_ref[...]
    packed = table[:, 0:1] * hidden[0:1, :]
    for r in range(1, ROWS):
        packed = packed + table[:, r : r + 1] * hidden[r : r + 1, :]
    for j, ref in enumerate((r0_ref, r1_ref, r2_ref, r3_ref)):
        ref[...] = packed[2 * j : 2 * j + 2, 0:FEAT]


def order_kernel(group_ref, after_ref, *refs):
    q_out, o_out, mark_ref = refs[8:]
    mark_ref[...] = jnp.zeros_like(mark_ref)
    for j in range(N_GRP):
        group = group_ref[0] ^ j
        q_out[:, pl.ds(pl.multiple_of(group * QW, LANES), QW)] = refs[j][...]
        o_out[:, pl.ds(pl.multiple_of(group * OW, LANES), OW)] = refs[N_GRP + j][...]


def call(kernel, outs, specs, scratch=(), vmem=32, flops=None):
    many = isinstance(outs, (list, tuple))
    return pl.pallas_call(
        kernel,
        out_shape=outs,
        in_specs=specs,
        out_specs=[VMEM] * len(outs) if many else VMEM,
        scratch_shapes=list(scratch),
        compiler_params=pltpu.CompilerParams(vmem_limit_bytes=vmem * MIB),
        cost_estimate=flops
        and pl.CostEstimate(flops=flops, bytes_accessed=4 * MIB, transcendentals=0),
    )


SWAP = [(0, 1), (1, 0)]


def to_groups(x):
    far = lax.ppermute(x, "xh", SWAP)
    return lax.ppermute(x, "core", SWAP), far, lax.ppermute(far, "core", SWAP)


def to_groups_at_once(x):
    return (
        lax.ppermute(x, "core", SWAP),
        lax.ppermute(x, "xh", SWAP),
        lax.ppermute(x, G_AXES, [(g, g ^ 3) for g in range(N_GRP)]),
    )


def exchange(x):
    rows = x.shape[0] // N_DEV
    x = x.reshape(N_DEV, rows, x.shape[1])
    x = lax.all_to_all(x, D_AXES, split_axis=0, concat_axis=0, tiled=True)
    return x.reshape(N_DEV * rows, x.shape[2])


def shards(hidden_in, w_qkv, w_o, key_cache, value_cache, lengths, finished, assignment):
    struct = jax.ShapeDtypeStruct
    group = lax.axis_index(G_AXES).astype(jnp.int32)
    dev = lax.axis_index(D_AXES).astype(jnp.int32)
    dev, group_one = dev.reshape(1), group.reshape(1)

    wq, wo = w_qkv.T, w_o.T
    far = lax.ppermute(wq, "xh", SWAP)
    both = lax.ppermute(jnp.stack([wq, far]), "core", SWAP)
    part = struct((N_DEV * ROWS, LANES), BF16)
    sent = call(
        pack_kernel,
        struct((N_DEV * PIECE, LANES), BF16),
        [SMEM] + [ANY] * 3,
        [
            pltpu.VMEM((ROWS, FEAT), BF16),
            pltpu.VMEM((WQ, D), BF16),
            pltpu.VMEM((WO, D), BF16),
            pltpu.VMEM((FULL, D), F32),
            pltpu.VMEM((MAIN, D), F32),
            pltpu.SemaphoreType.DMA((5,)),
        ],
        vmem=60,
    )(dev, hidden_in, wq, wo)
    recv = exchange(sent)
    merged = call(merge_kernel, struct((LANES, D), BF16), [VMEM] * 3)(wq, far, both)
    sent = call(project_kernel, part, [SMEM, SMEM, VMEM, VMEM])(dev, group_one, recv, merged)
    got = exchange(sent)

    o_block, lengths = call(
        turn_o_kernel,
        [struct((FEAT, OW), BF16), struct((ROWS, LANES), jnp.int32)],
        [SMEM, SMEM, VMEM, ANY],
        [pltpu.VMEM((OW, LANES), F32)],
    )(dev, lengths, recv, sent)
    o_blocks = (o_block,) + to_groups(o_block)

    q_block = call(
        turn_q_kernel,
        struct((FEAT, QW), BF16),
        [SMEM, VMEM, ANY],
        [pltpu.VMEM((QW, LANES), F32)],
    )(dev, recv, sent)
    q_blocks = (q_block,) + to_groups(q_block)
    cache = (ROWS * POS, KV_HEADS * LANES)
    tall = struct((KV_HEADS * GROUP, LANES), F32)
    tiles = call(
        query_kernel, struct(((HEADS + 2 * KV_HEADS) * ROWS, LANES), F32), [VMEM], flops=10**10
    )(got)
    scored = call(
        score_kernel,
        [struct((KV_HEADS * WIDE, ROWS * POS), BF16), tall, tall]
        + [struct((KV_HEADS * ROWS, LANES), F32)],
        [SMEM] + [VMEM] * 3,
        flops=10**10,
    )(dev, lengths, tiles, key_cache.reshape(cache))
    sent = call(value_kernel, part, [VMEM] * 5, flops=10**10)(*scored, value_cache.reshape(cache))
    got = exchange(sent)
    sent = call(finish_kernel, part, [SMEM, SMEM] + [VMEM] * 5)(
        dev, group_one, got, *o_blocks
    )
    w_qkv_gen, w_o_gen, mark = call(
        order_kernel,
        [
            struct((FEAT, N_GRP * QW), BF16),
            struct((FEAT, N_GRP * OW), BF16),
            struct((ROWS, LANES), F32),
        ],
        [SMEM, ANY] + [VMEM] * 8,
    )(group_one, sent, *q_blocks, *o_blocks)
    got = exchange(sent)

    learners = jnp.arange(N_GRP, dtype=jnp.int32) ^ group
    matches = (assignment[None, :] == learners[:, None]) & (finished[None, :] == 1)
    ranks = jnp.cumsum(matches.astype(jnp.int32), axis=1)
    slots = jnp.arange(1, 3, dtype=jnp.int32)
    table = matches[:, None, :] & (ranks[:, None, :] == slots[None, :, None])
    table = table.reshape(ROWS, ROWS).astype(F32)
    few = struct((2, FEAT), F32)
    hidden_out, r0, r1, r2, r3 = call(
        total_kernel, [struct((ROWS, FEAT), F32)] + [few] * 4, [SMEM, VMEM, VMEM, ANY]
    )(dev, table, got, mark)
    r1 = lax.ppermute(r1, "core", SWAP)
    r2 = lax.ppermute(r2, "xh", SWAP)
    r3 = lax.ppermute(r3, G_AXES, [(g, g ^ 3) for g in range(N_GRP)])
    returned = jnp.concatenate(swapped_blocks((r0, r1, r2, r3), group), axis=0)
    return (hidden_out, returned, w_qkv_gen, w_o_gen)


def solution(mesh):
    fine = Mesh(mesh.devices.reshape(2, 2, 2, 4, 8), G_AXES + D_AXES)
    return jax.shard_map(
        shards,
        mesh=fine,
        in_specs=(
            P(G_AXES, D_AXES),
            P(None, G_AXES + D_AXES),
            P(None, G_AXES + D_AXES),
            P(G_AXES, D_AXES, None),
            P(G_AXES, D_AXES, None),
            P(G_AXES),
            P(G_AXES),
            P(G_AXES),
        ),
        out_specs=(P(G_AXES, D_AXES), P(G_AXES, D_AXES), P(D_AXES, None), P(D_AXES, None)),
        check_vma=False,
    )
```
